32 devices in a mesh: section: 2 (over core), dp: 16 (over z, y, x).
Axes of the slice: x: 2, y: 2, z: 4, core: 2. Of those that a mesh axis runs over, the one named last changes fastest.
Arguments:
- inputs: bfloat16 [2, 16, 1024, 1024], P(None, 'dp'), may hold values from -6 to 6
- cotangent: bfloat16 [2, 16, 1024, 1024], P(None, 'dp'), may hold values from -6 to 6
- doc_lengths: int32 [2, 16, 8], P(None, 'dp'), may hold values from 1 to 512, 1024 in all within a row
- attend_gain: bfloat16 [2, 1024], P('section'), may hold values from 0.5 to 1.5
- attend_bias: bfloat16 [2, 1024], P('section'), may hold values from -1.796875 to 1.796875
- mixing_weight: bfloat16 [2, 1024, 3072], P('section'), may hold values from -0.1875 to 0.1875
- mixing_bias: bfloat16 [2, 3072], P('section'), may hold values from -1.796875 to 1.796875
- output_weight: bfloat16 [2, 1024, 1024], P('section'), may hold values from -0.75 to 0.75
- output_bias: bfloat16 [2, 1024], P('section'), may hold values from -1.796875 to 1.796875
- feed_gain: bfloat16 [2, 1024], P('section'), may hold values from 0.5 to 1.5
- feed_bias: bfloat16 [2, 1024], P('section'), may hold values from -1.796875 to 1.796875
- expand_weight: bfloat16 [2, 1024, 4096], P('section'), may hold values from -0.1875 to 0.1875
- expand_bias: bfloat16 [2, 4096], P('section'), may hold values from -1.796875 to 1.796875
- reduce_weight: bfloat16 [2, 4096, 1024], P('section'), may hold values from -0.1875 to 0.1875
- reduce_bias: bfloat16 [2, 1024], P('section'), may hold values from -1.796875 to 1.796875
- prefix_embed: bfloat16 [10, 1024], replicated, may hold values from -6 to 6
- hidden_weight: bfloat16 [1024, 512], replicated, may hold values from -0.1875 to 0.1875
- hidden_bias: bfloat16 [512], replicated, may hold values from -3 to 3
- prefix_weight: bfloat16 [2, 512, 2048], P('section', None, 'dp'), may hold values from -0.5 to 0.5
- prefix_bias: bfloat16 [2, 2048], P('section', 'dp'), may hold values from -1.796875 to 1.796875
Outputs:
- layer_out: bfloat16 [2, 2, 16, 1024, 1024], P('section', None, 'dp')
- input_grad: bfloat16 [2, 2, 16, 1024, 1024], P('section', None, 'dp')
- grad_embed: float32 [10, 1024], replicated
- grad_hidden_weight: float32 [1024, 512], replicated
- grad_hidden_bias: float32 [512], replicated
- grad_prefix_weight: float32 [2, 512, 2048], P('section', None, 'dp')
- grad_prefix_bias: float32 [2, 2048], P('section', 'dp')
The draws below stay inside these ranges and needn't reach their ends.
Inputs may be any that keep to these rules, and one draw needn't show every extreme that they name: `doc_lengths`: each sequence's 8 lengths sum to 1024; the longest of them is exactly 512.
All inputs are finite; a program needn't handle non-finite values.
Results may differ from the reference program's by a relative error of at most 0.018.
Values may be sent and summed in bfloat16 or wider, within the bound.
No kernel may reach another device: no remote copies, remote signals or barrier semaphores. Data moves between devices by JAX's collectives and lax.ppermute only.
A program may use at most 320 MiB of HBM per device.

```python
import math
import jax
import jax.numpy as jnp
import numpy as np
from jax import lax

D = 1024
HEADS = 16
HEAD_DIM = 64
FF = 4096
HIDDEN_SIZE = 512
PRE = 10
LENGTH = 1024
DOCS = 8
BLOCK = 512
MICRO = 2
BATCH = 16
LAYERS = 2


def levels(stream_key, extent, shards, least, top_value):
    factor_of, own = 1.0, jax.random.fold_in(stream_key, 6)
    for dim, shards_of in shards:
        steps = jnp.exp(jax.random.uniform(jax.random.fold_in(own, dim), (shards_of,), jnp.float32, least / len(shards), top_value / len(shards)))
        factor_of = factor_of * jnp.repeat(steps, extent[dim] // shards_of).reshape([-1 if axis == dim else 1 for axis in range(len(extent))])
    return factor_of


def profile(count, total, most, slope):
    loads = [(1 << 20) // math.isqrt(grade ** slope) + 1 for grade in range(2, count + 1)]
    spare, holding = total - most - (count - 1), [1] * (count - 1)
    while spare > 0:
        candidates = [i for i in range(count - 1) if holding[i] < most]
        mass, budget = sum([loads[i] for i in candidates]), spare
        for i in candidates:
            extra = min(most - holding[i], max(1, budget * loads[i] // mass), spare)
            holding[i] = holding[i] + extra
            spare = spare - extra
    return np.array([most] + holding)


def uneven(rng, count, total, most, skew):
    if count == 2:
        one = jax.random.randint(rng, (), max(1, total - most), min(most, total - 1) + 1)
        return jnp.stack([one, total - one])
    sizes = jnp.asarray(profile(count, total, most, skew), jnp.int32)
    couples = (count - 1) // 2
    giver, receiver = sizes[1:1 + 2 * couples:2], sizes[2:2 + 2 * couples:2]
    slack = jnp.minimum(giver - 1, most - receiver)
    passed = jax.random.randint(jax.random.fold_in(rng, 1), (couples,), 0, 1 << 20) % (slack + 1)
    sizes = sizes.at[1:1 + 2 * couples:2].set(giver - passed).at[2:2 + 2 * couples:2].set(receiver + passed)
    return sizes[jax.random.permutation(jax.random.fold_in(rng, 2), count)]


def gaussian(stream_key, dims, spread, most, pieces=(), held_as=jnp.bfloat16):
    level = levels(stream_key, dims, pieces, -0.22, 0.18) if pieces else 1.0
    result = jax.random.normal(stream_key, dims, jnp.float32) * spread * level
    return jnp.minimum(jnp.maximum(result, -most), most).astype(held_as)


def setup_inputs(seed: int = 0) -> dict:
    splits = jax.random.split(jax.random.key(seed), 21)
    return {
        "inputs": gaussian(splits[0], (MICRO, BATCH, LENGTH, D), 1.0, 6.0, ((1, 16),)),
        "cotangent": gaussian(splits[1], (MICRO, BATCH, LENGTH, D), 1.0, 6.0, ((1, 16),)),
        "doc_lengths": jax.vmap(lambda own: uneven(own, DOCS, LENGTH, LENGTH // 2, 2))(jax.random.split(splits[2], MICRO * BATCH)).reshape((MICRO, BATCH, DOCS)).astype(jnp.int32),
        "attend_gain": jnp.clip(1.0 + 0.1 * jax.random.normal(splits[3], (LAYERS, D), jnp.float32), 0.5, 1.5).astype(jnp.bfloat16),
        "attend_bias": gaussian(splits[4], (LAYERS, D), 0.3, 1.796875, ((0, 2),)),
        "mixing_weight": gaussian(splits[5], (LAYERS, D, 3 * D), D ** -0.5, 0.1875, ((0, 2),)),
        "mixing_bias": gaussian(splits[6], (LAYERS, 3 * D), 0.3, 1.796875, ((0, 2),)),
        "output_weight": gaussian(splits[7], (LAYERS, D, D), (D // 16) ** -0.5, 0.75, ((0, 2),)),
        "output_bias": gaussian(splits[8], (LAYERS, D), 0.3, 1.796875, ((0, 2),)),
        "feed_gain": jnp.clip(1.0 + 0.1 * jax.random.normal(splits[9], (LAYERS, D), jnp.float32), 0.5, 1.5).astype(jnp.bfloat16),
        "feed_bias": gaussian(splits[10], (LAYERS, D), 0.3, 1.796875, ((0, 2),)),
        "expand_weight": gaussian(splits[11], (LAYERS, D, FF), D ** -0.5, 0.1875, ((0, 2),)),
        "expand_bias": gaussian(splits[12], (LAYERS, FF), 0.3, 1.796875, ((0, 2),)),
        "reduce_weight": gaussian(splits[13], (LAYERS, FF, D), (FF // 4) ** -0.5, 0.1875, ((0, 2),)),
        "reduce_bias": gaussian(splits[14], (LAYERS, D), 0.3, 1.796875, ((0, 2),)),
        "prefix_embed": gaussian(splits[15], (PRE, D), 1.0, 6.0),
        "hidden_weight": gaussian(splits[16], (D, HIDDEN_SIZE), D ** -0.5, 0.1875),
        "hidden_bias": gaussian(splits[17], (HIDDEN_SIZE,), 0.5, 3.0),
        "prefix_weight": gaussian(splits[18], (LAYERS, HIDDEN_SIZE, 2 * D), (HIDDEN_SIZE // 4) ** -0.5, 0.5, ((0, 2), (2, 16))),
        "prefix_bias": gaussian(splits[19], (LAYERS, 2 * D), 0.3, 1.796875, ((0, 2), (1, 16))),
    }


@jax.custom_vjp
def low(v):
    return lax.optimization_barrier(v.astype(jnp.bfloat16)).astype(jnp.float32)

@jax.custom_vjp
def low_back(v):
    return v

def low_keep(v):
    return (low(v), None)

def low_pass(kept, grad):
    return (grad,)

def back_keep(v):
    return (v, None)

def back_low(kept, grad):
    return (low(grad),)
low.defvjp(low_keep, low_pass)
low_back.defvjp(back_keep, back_low)
masked_score = -1000000000.0

def matmul(left, right):
    return jnp.dot(left, right, precision=lax.Precision.HIGHEST)

def norm_apply(values, gain, offset):
    centre = lax.optimization_barrier(jnp.mean(values, axis=-1, keepdims=True))
    shifted = values - centre
    variance = lax.optimization_barrier(jnp.mean(shifted * shifted, axis=-1, keepdims=True))
    return shifted * lax.rsqrt(variance + 1e-05) * gain + offset

def document_ids(lengths):
    doc_ends = jnp.cumsum(lengths, axis=-1).astype(jnp.int32)[..., :-1]
    places = jnp.arange(LENGTH, dtype=jnp.int32)
    return lax.optimization_barrier(jnp.sum((places[:, None] >= doc_ends[..., None, :]).astype(jnp.int32), axis=-1)).astype(jnp.int32)

def attend(queries, key_part, value_part, prefix_keys, prefix_values, doc_ids):
    score_scale = HEAD_DIM ** (-0.5)
    all_keys = jnp.concatenate([prefix_keys, key_part], 0).reshape(PRE + LENGTH, HEADS, HEAD_DIM)
    all_values = jnp.concatenate([prefix_values, value_part], 0).reshape(PRE + LENGTH, HEADS, HEAD_DIM)
    block_count = LENGTH // BLOCK
    query_blocks = queries.reshape(block_count, BLOCK, HEADS, HEAD_DIM)
    block_starts = jnp.arange(block_count, dtype=jnp.int32) * BLOCK
    columns = jnp.arange(LENGTH, dtype=jnp.int32)

    def one_block(item_pair):
        query_rows, start_row = item_pair
        places = start_row + jnp.arange(BLOCK, dtype=jnp.int32)
        row_ids = lax.dynamic_slice_in_dim(doc_ids, start_row.astype(jnp.int32), BLOCK)
        visible = (columns[None, :] <= places[:, None]) & (doc_ids[None, :] == row_ids[:, None])
        visible = jnp.concatenate([jnp.ones((BLOCK, PRE), dtype=jnp.bool_), visible], 1)
        scores = jnp.einsum('qhd,khd->hqk', query_rows, all_keys, precision=lax.Precision.HIGHEST) * score_scale
        scores = low_back(jnp.where(visible[None], scores, masked_score))
        totals = jax.nn.logsumexp(scores, axis=-1, keepdims=True)
        probabilities = low(jnp.exp(scores - totals))
        return jnp.einsum('hqk,khd->qhd', probabilities, all_values, precision=lax.Precision.HIGHEST)
    results = lax.map(jax.checkpoint(one_block), (query_blocks, block_starts))
    return results.reshape(LENGTH, HEADS * HEAD_DIM)

def run_layer(hidden, layer_weights, table, doc_ids):
    attend_gain, attend_bias, mixing_weight, mixing_bias, output_weight, output_bias, feed_gain, feed_bias, expand_weight, expand_bias, reduce_weight, reduce_bias = layer_weights
    normed = low(norm_apply(hidden, attend_gain, attend_bias))
    mixed = low(low_back(matmul(normed, mixing_weight) + mixing_bias))
    queries = mixed[:, :D]
    key_part = mixed[:, D:2 * D]
    value_part = mixed[:, 2 * D:]
    attended = low(low_back(attend(queries, key_part, value_part, table[:, :D], table[:, D:], doc_ids)))
    branch = low_back(matmul(attended, output_weight) + output_bias)
    middle = hidden + branch
    second = low(norm_apply(middle, feed_gain, feed_bias))
    expanded = low_back(matmul(second, expand_weight) + expand_bias)
    activated = low(jax.nn.gelu(expanded, approximate=True))
    branch_two = low_back(matmul(activated, reduce_weight) + reduce_bias)
    return middle + branch_two

def reference(inputs, cotangent, doc_lengths, attend_gain, attend_bias, mixing_weight, mixing_bias, output_weight, output_bias, feed_gain, feed_bias, expand_weight, expand_bias, reduce_weight, reduce_bias, prefix_embed, hidden_weight, hidden_bias, prefix_weight, prefix_bias):
    sequences = MICRO * BATCH
    flat_inputs = inputs.astype(jnp.float32).reshape(sequences, LENGTH, D)
    flat_ids = document_ids(doc_lengths.reshape(sequences, DOCS))
    extras = jnp.zeros((sequences, LAYERS - 1, LENGTH, D), jnp.float32)
    stacked = tuple((weight.astype(jnp.float32) for weight in (attend_gain, attend_bias, mixing_weight, mixing_bias, output_weight, output_bias, feed_gain, feed_bias, expand_weight, expand_bias, reduce_weight, reduce_bias)))

    def forward(flat_values, nudges_all, embed, first_weight, first_bias, second_weight, second_bias):
        activity = jnp.tanh(matmul(embed, first_weight) + first_bias)
        activity_low = low(activity)
        tables = [low(matmul(activity_low, second_weight[layer_index]) + second_bias[layer_index]) for layer_index in range(LAYERS)]

        def one_sequence(item):
            hidden, seq_ids, nudges = item
            results = []
            for layer_index in range(LAYERS):
                layer_weights = tuple((weight[layer_index] for weight in stacked))
                hidden = run_layer(hidden, layer_weights, tables[layer_index], seq_ids)
                if layer_index < LAYERS - 1:
                    hidden = low_back(low(hidden + nudges[layer_index]))
                else:
                    hidden = low(hidden)
                results.append(hidden)
            return jnp.stack(results)
        return lax.map(jax.checkpoint(one_sequence), (flat_values, flat_ids, nudges_all))
    primals = (flat_inputs, extras, prefix_embed.astype(jnp.float32), hidden_weight.astype(jnp.float32), hidden_bias.astype(jnp.float32), prefix_weight.astype(jnp.float32), prefix_bias.astype(jnp.float32))
    outputs, pullback = jax.vjp(forward, *primals)
    seed_grad = jnp.zeros_like(outputs).at[:, LAYERS - 1].set(cotangent.astype(jnp.float32).reshape(sequences, LENGTH, D))
    gradients = pullback(seed_grad)
    layer_out = outputs.reshape(MICRO, BATCH, LAYERS, LENGTH, D).transpose(2, 0, 1, 3, 4).astype(jnp.bfloat16)
    leading = gradients[0][:, None]
    every_grad = jnp.concatenate([leading, gradients[1]], 1)
    input_grad = every_grad.reshape(MICRO, BATCH, LAYERS, LENGTH, D).transpose(2, 0, 1, 3, 4).astype(jnp.bfloat16)
    return (layer_out, input_grad, gradients[2], gradients[3], gradients[4], gradients[5], gradients[6])
```

```python
import jax
import jax.numpy as jnp
from jax import lax
from jax.experimental import pallas as pl
from jax.experimental.pallas import tpu as pltpu
from jax.sharding import PartitionSpec as P

F32 = jnp.float32
BF = jnp.bfloat16
LENGTH = 1024
WIDTH = 1024
FF = 4096
HEADS = 16
PRE = 10
PAD = 16
DOCS = 8
QB = 128
KC = 128
PAIRS = 8
STEPS = 5
NEG = -1e9
C0 = 0.7978845608028654
C1 = C0 * 0.044715

ANY = pl.BlockSpec(memory_space=pl.ANY)
SMEM = pl.BlockSpec(memory_space=pltpu.SMEM)
VMEM = pl.BlockSpec(memory_space=pltpu.VMEM)


def dot(a, b):
    return jnp.dot(a, b, preferred_element_type=F32)


def dot_nt(a, b):
    return lax.dot_general(a, b, (((1,), (1,)), ((), ())), preferred_element_type=F32)


def dot_tn(a, b):
    return lax.dot_general(a, b, (((0,), (0,)), ((), ())), preferred_element_type=F32)


def split(value):
    high = value.astype(BF)
    return high, (value - high.astype(F32)).astype(BF)


def call(kernel, ins, in_specs, outs, scratch, name, flops=0, moved=0, out_specs=None):
    return pl.pallas_call(
        kernel,
        in_specs=in_specs,
        out_specs=out_specs or [ANY] * len(outs),
        out_shape=[jax.ShapeDtypeStruct(s, d) for s, d in outs],
        scratch_shapes=scratch,
        compiler_params=pltpu.CompilerParams(vmem_limit_bytes=60 << 20),
        cost_estimate=pl.CostEstimate(flops=flops, bytes_accessed=moved, transcendentals=0),
        name=name,
    )(*ins)


class Copy:
    def __init__(self, source, target, sem, other=None, own=None):
        self.first = pltpu.make_async_copy(source, target, sem)
        self.second = None if other is None else pltpu.make_async_copy(other, target, sem)
        self.own = own

    def start(self):
        if self.second is None:
            self.first.start()
        else:
            pl.when(self.own)(self.first.start)
            pl.when(jnp.logical_not(self.own))(self.second.start)
        return self

    def wait(self):
        self.first.wait()


class Sems:
    def __init__(self, ref):
        self.ref = ref
        self.used = 0

    def __call__(self):
        self.used += 1
        return self.ref.at[self.used - 1]


GAIN_A, BIAS_A, BIAS_M, BIAS_O, GAIN_F, BIAS_F, BIAS_E, BIAS_R = 0, 1, 2, 5, 6, 7, 8, 12


def tile(index, rows):
    return slice(index * rows, (index + 1) * rows)


def normalise(values):
    centre = jnp.mean(values, axis=-1, keepdims=True)
    shifted = values - centre
    variance = jnp.mean(shifted * shifted, axis=-1, keepdims=True)
    scale = lax.rsqrt(variance + 1e-5)
    return shifted * scale, scale


def norm_back(grad, gain, hat, scale):
    weighted = grad * gain
    first = jnp.mean(weighted, axis=-1, keepdims=True)
    second = jnp.mean(weighted * hat, axis=-1, keepdims=True)
    return scale * (weighted - first - hat * second)


def document_ends(lens, row):
    ends, total = [], None
    for doc in range(DOCS - 1):
        total = lens[row, doc] if total is None else total + lens[row, doc]
        ends.append(total)
    return ends


def window(ends, block):
    first = block * QB
    low = jnp.int32(0)
    for end in ends:
        low = jnp.maximum(low, jnp.where(first >= end, end, 0))
    count = (first + QB - low + KC - 1) // KC
    start = jnp.maximum(first + QB - count * KC, 0)
    return first, count, start


def visible(ends, first, start, count):
    places = first + lax.broadcasted_iota(jnp.int32, (1, QB), 1)
    low = jnp.zeros((1, QB), jnp.int32)
    for end in ends:
        low = jnp.maximum(low, jnp.where(places >= end, end, 0))
    keys = start + lax.broadcasted_iota(jnp.int32, (count * KC, QB), 0)
    inside = jnp.where((keys <= places) & (keys >= low), 0.0, NEG).astype(F32)
    prefix = lax.broadcasted_iota(jnp.int32, (PAD, QB), 0)
    prefix = jnp.where(prefix < PRE, 0.0, NEG).astype(F32)
    mask = jnp.concatenate([prefix, inside], 0)
    return jnp.concatenate([mask, mask], 1)


def spread(block):
    lane = lax.broadcasted_iota(jnp.int32, block.shape, 1) // 64
    zero = jnp.zeros_like(block)
    return jnp.concatenate([jnp.where(lane == h, block, zero) for h in range(2)], 0)


def gather_heads(block):
    both = [block[h * 64 : h * 64 + 64, h * QB : h * QB + QB] for h in range(2)]
    return jnp.concatenate(both, 0).T


def columns(pair, third):
    return slice(third * WIDTH + pair * 128, third * WIDTH + pair * 128 + 128)


def attend_step(refs, ends, first, start, count, block):
    mixed, table, attended, totals = refs
    mask = visible(ends, first, start, count)
    rows = pl.ds(pl.multiple_of(first, QB), QB)
    keys = pl.ds(pl.multiple_of(start, QB), count * KC)
    lanes = pl.ds(pl.multiple_of(first, QB), QB)
    pairs = range(PAIRS)
    scores = [
        dot_nt(
            jnp.concatenate([table[:, columns(p, 0)], mixed[keys, columns(p, 1)]], 0),
            spread(mixed[rows, columns(p, 0)]),
        )
        + mask
        for p in pairs
    ]
    tops = [jnp.max(s, 0, keepdims=True) for s in scores]
    raised = [jnp.exp(s - t) for s, t in zip(scores, tops)]
    sums = [jnp.sum(r, 0, keepdims=True) for r in raised]
    low = [r.astype(BF) for r in raised]
    outs = [
        dot_tn(
            jnp.concatenate([table[:, columns(p, 1)], mixed[keys, columns(p, 2)]], 0), low[p]
        )
        for p in pairs
    ]
    for p in pairs:
        log_total = tops[p] + jnp.log(sums[p])
        for h in range(2):
            totals[pl.ds(2 * p + h, 1), lanes] = log_total[:, h * QB : h * QB + QB]
        attended[rows, columns(p, 0)] = gather_heads(outs[p] * (1.0 / sums[p])).astype(BF)


def attend(mixed, table, lens, row, attended, totals):
    ends = document_ends(lens, row)

    def step(block, carry):
        first, count, start = window(ends, block)
        for size in range(1, STEPS + 1):

            @pl.when(count == size)
            def _():
                attend_step((mixed, table, attended, totals), ends, first, start, size, block)

        return carry

    lax.fori_loop(0, LENGTH // QB, step, 0)


def attend_back_step(refs, ends, first, start, count, block):
    mixed, grad_out, totals, centres, table, grad_mixed, key_sum, value_sum = refs
    mask = visible(ends, first, start, count)
    rows = pl.ds(pl.multiple_of(first, QB), QB)
    keys = pl.ds(pl.multiple_of(start, QB), count * KC)
    lanes = pl.ds(pl.multiple_of(first, QB), QB)
    pairs = range(PAIRS)

    def row_of(ref, p):
        return jnp.concatenate([ref[pl.ds(2 * p + h, 1), lanes] for h in range(2)], 1)

    queries = [spread(mixed[rows, columns(p, 0)]) for p in pairs]
    grads = [spread(grad_out[rows, columns(p, 0)]) for p in pairs]
    all_keys = [
        jnp.concatenate([table[:, columns(p, 0)], mixed[keys, columns(p, 1)]], 0) for p in pairs
    ]
    all_values = [
        jnp.concatenate([table[:, columns(p, 1)], mixed[keys, columns(p, 2)]], 0) for p in pairs
    ]
    scores = [dot_nt(all_keys[p], queries[p]) for p in pairs]
    grad_probs = [dot_nt(all_values[p], grads[p]) for p in pairs]
    probs = [jnp.exp(scores[p] + (mask - row_of(totals, p))) for p in pairs]
    low = [p.astype(BF) for p in probs]
    value_grads = [dot(low[p][PAD:], grads[p]) for p in pairs]
    grad_scores = [(probs[p] * (grad_probs[p] - row_of(centres, p))).astype(BF) for p in pairs]
    key_grads = [dot(grad_scores[p][PAD:], queries[p]) for p in pairs]
    query_grads = [dot_tn(all_keys[p], grad_scores[p]) for p in pairs]
    for p in pairs:
        grad_mixed[rows, columns(p, 0)] = (gather_heads(query_grads[p]) * 0.125).astype(BF)
        value_sum[keys, columns(p, 0)] += value_grads[p]
        key_sum[keys, columns(p, 0)] += key_grads[p]


def attend_back(mixed, grad_out, totals, centres, table, lens, row, grad_mixed, sums):
    ends = document_ends(lens, row)
    key_sum, value_sum = sums

    def clear(index, carry):
        rows = pl.ds(pl.multiple_of(index * 64, 64), 64)
        key_sum[rows, :] = jnp.zeros((64, WIDTH), F32)
        value_sum[rows, :] = jnp.zeros((64, WIDTH), F32)
        return carry

    lax.fori_loop(0, LENGTH // 64, clear, 0)

    def step(block, carry):
        first, count, start = window(ends, block)
        for size in range(1, STEPS + 1):

            @pl.when(count == size)
            def _():
                refs = (mixed, grad_out, totals, centres, table, grad_mixed, key_sum, value_sum)
                attend_back_step(refs, ends, first, start, size, block)

        return carry

    lax.fori_loop(0, LENGTH // QB, step, 0)

    def finish(index, carry):
        rows = pl.ds(pl.multiple_of(index * 64, 64), 64)
        grad_mixed[rows, WIDTH : 2 * WIDTH] = key_sum[rows, :].astype(BF)
        grad_mixed[rows, 2 * WIDTH :] = value_sum[rows, :].astype(BF)
        return carry

    lax.fori_loop(0, LENGTH // 64, finish, 0)


def prefix_back(queries, grad_out, attended, totals, centres, table, grad_table):
    heads = lax.broadcasted_iota(jnp.int32, (HEADS, WIDTH), 0)
    lanes = lax.broadcasted_iota(jnp.int32, (HEADS, WIDTH), 1)
    pick = jnp.where(lanes // 64 == heads, 1.0, 0.0).astype(BF)
    high, low = split(attended[...].astype(F32) * grad_out[...].astype(F32))
    centre = dot_nt(pick, high) + dot_nt(pick, low)
    centres[...] = centre
    real = lax.broadcasted_iota(jnp.int32, (4 * PAD, LENGTH), 0) % PAD < PRE
    lane = lax.broadcasted_iota(jnp.int32, (PAD, 256), 1) // 64

    def widen(block):
        zero = jnp.zeros_like(block)
        return jnp.concatenate([jnp.where(lane == h, block, zero) for h in range(4)], 0)

    def narrow(block):
        result = block[:PAD]
        for h in range(1, 4):
            result = jnp.where(lane == h, block[h * PAD : (h + 1) * PAD], result)
        return result

    def repeat(rows):
        return jnp.concatenate(
            [jnp.broadcast_to(rows[h : h + 1], (PAD, LENGTH)) for h in range(4)], 0
        )

    for quad in range(4):
        cols = slice(quad * 256, quad * 256 + 256)
        later = slice(WIDTH + quad * 256, WIDTH + quad * 256 + 256)
        mine = slice(quad * 4, quad * 4 + 4)
        scores = dot_nt(widen(table[:, cols]), queries[:, cols]) - repeat(totals[mine, :])
        probs = jnp.where(real, jnp.exp(scores), 0.0)
        grad_probs = dot_nt(widen(table[:, later]), grad_out[:, cols])
        grad_scores = (probs * (grad_probs - repeat(centre[mine, :]))).astype(BF)
        grad_table[:, cols] = narrow(dot(grad_scores, queries[:, cols]))
        grad_table[:, later] = narrow(dot(probs.astype(BF), grad_out[:, cols]))


def vm(shape, dtype=BF):
    return pltpu.VMEM(shape, dtype)


DMA = pltpu.SemaphoreType.DMA


def mix_kernel(layer):
    def kernel(sec, x, pack, pack2, w, w2, mixed, x_v, n_v, w_v, p_v, m_v, sems):
        own = sec[0] == layer
        sem = Sems(sems)
        source = x.at[sec[0]] if layer == 0 else x
        packs = Copy(pack, p_v, sem(), pack2, own).start()
        xs = [Copy(source.at[tile(r, 256)], x_v.at[tile(r, 256)], sem()).start() for r in range(4)]
        ws = [
            Copy(
                w.at[:, tile(j, WIDTH)], w_v.at[:, tile(j, WIDTH)], sem(),
                w2.at[:, tile(j, WIDTH)], own,
            ).start()
            for j in range(3)
        ]
        packs.wait()
        gain, bias = p_v[GAIN_A : GAIN_A + 1], p_v[BIAS_A : BIAS_A + 1]

        def norm(r):
            xs[r].wait()
            hat, _ = normalise(x_v[tile(r, 256)].astype(F32))
            n_v[tile(r, 256)] = (hat * gain + bias).astype(BF)

        norm(0)
        outs = []
        for j in range(3):
            ws[j].wait()
            cols = tile(j, WIDTH)
            for r in range(4):
                value = dot(n_v[tile(r, 256)], w_v[:, cols]) + p_v[BIAS_M + j : BIAS_M + j + 1]
                value = value.astype(BF)
                if j == 0:
                    value = value * jnp.asarray(0.125, BF)
                    if r < 3:
                        norm(r + 1)
                m_v[tile(r, 256), cols] = value
            outs.append(Copy(m_v.at[:, cols], mixed.at[:, cols], sem()).start())
        for out in outs:
            out.wait()

    return kernel


def mix(layer, sec, x, packs, weights):
    return call(
        mix_kernel(layer),
        (sec, x, *packs, *weights),
        [SMEM] + [ANY] * 5,
        [((LENGTH, 3 * WIDTH), BF)],
        [
            vm((LENGTH, WIDTH)), vm((LENGTH, WIDTH)), vm((WIDTH, 3 * WIDTH)), vm((16, 1024), F32),
            vm((LENGTH, 3 * WIDTH)), DMA((16,)),
        ],
        f"mix{layer}", 2 * LENGTH * WIDTH * 3 * WIDTH, 14 << 20,
    )[0]


def gelu_both(value):
    square = value * value
    half = 0.5 * jnp.tanh(value * (C1 * square + C0)) + 0.5
    result = value * half
    return result, half + result * (1.0 - half) * ((6 * C1) * square + 2 * C0)


def attend_kernel(layer):
    def kernel(
        sec, lens, x, mixed, table, pack, pack2, wo, wo2, we, we2,
        attended, totals, middle, slope, active,
        x_v, m_v, t_v, p_v, wo_v, we_v, at_v, to_v, mid_v, s_v, a_v, sems,
    ):
        own = sec[0] == layer
        sem = Sems(sems)
        source = x.at[sec[0]] if layer == 0 else x
        first = [Copy(mixed, m_v, sem()).start(), Copy(table, t_v, sem()).start()]
        packs = Copy(pack, p_v, sem(), pack2, own).start()
        later = [Copy(source, x_v, sem()).start(), Copy(wo, wo_v, sem(), wo2, own).start()]
        wes = [
            Copy(
                we.at[:, tile(j, 1024)], we_v.at[:, tile(j, 1024)], sem(),
                we2.at[:, tile(j, 1024)], own,
            ).start()
            for j in range(4)
        ]
        for copy in first:
            copy.wait()
        attend(m_v, t_v, lens, sec[0], at_v, to_v)
        outs = [Copy(at_v, attended, sem()).start(), Copy(to_v, totals, sem()).start()]
        for copy in later:
            copy.wait()
        packs.wait()
        gain, bias = p_v[GAIN_F : GAIN_F + 1], p_v[BIAS_F : BIAS_F + 1]
        seconds = []
        for r in range(4):
            rows = tile(r, 256)
            value = x_v[rows].astype(F32) + dot(at_v[rows], wo_v[...]) + p_v[BIAS_O : BIAS_O + 1]
            mid_v[rows] = value
            hat, _ = normalise(value)
            x_v[rows] = (hat * gain + bias).astype(BF)
        outs.append(Copy(mid_v, middle, sem()).start())
        for j in range(4):
            wes[j].wait()
        for r in range(2):
            rows = tile(r, 512)
            for j in range(8):
                cols = tile(j, 512)
                part = slice((j % 2) * 512, (j % 2) * 512 + 512)
                row = BIAS_E + j // 2
                value = dot(x_v[rows], we_v[:, cols]) + p_v[row : row + 1, part]
                result, derivative = gelu_both(value)
                a_v[rows, cols] = result.astype(BF)
                s_v[rows, cols] = derivative.astype(BF)
            outs.append(Copy(a_v.at[rows], active.at[rows], sem()).start())
            outs.append(Copy(s_v.at[rows], slope.at[rows], sem()).start())
        for out in outs:
            out.wait()

    return kernel


def attend_expand(layer, sec, lens, x, mixed, table, packs, wo, we):
    return call(
        attend_kernel(layer),
        (sec, lens, x, mixed, table, *packs, *wo, *we),
        [SMEM, SMEM] + [ANY] * 9,
        [
            ((LENGTH, WIDTH), BF), ((HEADS, LENGTH), F32), ((LENGTH, WIDTH), F32),
            ((LENGTH, FF), BF), ((LENGTH, FF), BF),
        ],
        [
            vm((LENGTH, WIDTH)), vm((LENGTH, 3 * WIDTH)), vm((PAD, 2 * WIDTH)), vm((16, 1024), F32),
            vm((WIDTH, WIDTH)), vm((WIDTH, FF)), vm((LENGTH, WIDTH)), vm((HEADS, LENGTH), F32),
            vm((LENGTH, WIDTH), F32), vm((LENGTH, FF)), vm((LENGTH, FF)), DMA((20,)),
        ],
        f"attend_expand{layer}", 2 * LENGTH * WIDTH * 8 * WIDTH, 44 << 20,
    )


def reduce_kernel(layer):
    def kernel(sec, active, middle, pack, pack2, wr, wr2, out, a_v, mid_v, p_v, w_v, o_v, sems):
        own = sec[0] == layer
        sem = Sems(sems)
        packs = Copy(pack, p_v, sem(), pack2, own).start()
        acts = [Copy(active.at[tile(0, 256)], a_v.at[tile(0, 256)], sem()).start()]
        mids = [Copy(middle, mid_v, sem())]
        ws = [
            Copy(
                wr.at[:, tile(n, 256)], w_v.at[:, tile(n, 256)], sem(),
                wr2.at[:, tile(n, 256)], own,
            ).start()
            for n in range(4)
        ]
        mids[0].start()
        for r in range(1, 4):
            acts.append(Copy(active.at[tile(r, 256)], a_v.at[tile(r, 256)], sem()).start())
        packs.wait()
        outs = []
        for r in range(4):
            rows = tile(r, 256)
            acts[r].wait()
            for n in range(4):
                cols = tile(n, 256)
                if r == 0:
                    ws[n].wait()
                value = dot(a_v[rows], w_v[:, cols]) + p_v[BIAS_R : BIAS_R + 1, cols]
                if r == 0 and n == 0:
                    mids[0].wait()
                o_v[rows, cols] = (mid_v[rows, cols] + value).astype(BF)
            outs.append(Copy(o_v.at[rows], out.at[rows], sem()).start())
        for copy in outs:
            copy.wait()

    return kernel


def reduce(layer, sec, active, middle, packs, wr):
    return call(
        reduce_kernel(layer),
        (sec, active, middle, *packs, *wr),
        [SMEM] + [ANY] * 6,
        [((LENGTH, WIDTH), BF)],
        [
            vm((LENGTH, FF)), vm((LENGTH, WIDTH), F32), vm((16, 1024), F32), vm((FF, WIDTH)),
            vm((LENGTH, WIDTH)), DMA((16,)),
        ],
        f"reduce{layer}", 2 * LENGTH * WIDTH * FF, 22 << 20,
    )[0]


def feed_back_kernel(layer):
    def kernel(
        sec, g, slope, middle, mixed, attended, totals, table, pack, pack2, wo, wo2, we, we2, wr, wr2,
        grad_middle, grad_out, centres, grad_table,
        g_v, s_v, mid_v, q_v, at_v, to_v, t_v, p_v, wo_v, we_v, wr_v, acc_v, go_v, c_v, gt_v, sems,
    ):
        own = sec[0] == layer
        sem = Sems(sems)
        source = g.at[sec[0]] if layer == 1 else g
        gs = Copy(source, g_v, sem()).start()
        parts = []
        for c in range(8):
            cols = tile(c, 512)
            parts.append([
                Copy(wr.at[cols], wr_v.at[cols], sem(), wr2.at[cols], own).start(),
                Copy(slope.at[:, cols], s_v.at[:, cols], sem()).start(),
                Copy(we.at[:, cols], we_v.at[:, cols], sem(), we2.at[:, cols], own).start(),
            ])
        packs = Copy(pack, p_v, sem(), pack2, own).start()
        mids = Copy(middle, mid_v, sem()).start()
        wos = Copy(wo, wo_v, sem(), wo2, own).start()
        later = [
            Copy(mixed.at[:, :WIDTH], q_v, sem()).start(),
            Copy(attended, at_v, sem()).start(),
            Copy(totals, to_v, sem()).start(),
            Copy(table, t_v, sem()).start(),
        ]
        gs.wait()
        for r in range(2):
            rows = tile(r, 512)
            total = None
            for c in range(8):
                cols = tile(c, 512)
                if r == 0:
                    for copy in parts[c]:
                        copy.wait()
                value = dot_nt(g_v[rows], wr_v[cols]) * s_v[rows, cols].astype(F32)
                value = dot_nt(value.astype(BF), we_v[:, cols])
                total = value if total is None else total + value
            acc_v[rows] = total
        packs.wait()
        mids.wait()
        wos.wait()
        gain = p_v[GAIN_F : GAIN_F + 1]
        outs = []
        for r in range(4):
            rows = tile(r, 256)
            hat, scale = normalise(mid_v[rows])
            value = g_v[rows].astype(F32) + norm_back(acc_v[rows], gain, hat, scale)
            acc_v[rows] = value
            go_v[rows] = dot_nt(value.astype(BF), wo_v[...]).astype(BF)
        outs.append(Copy(acc_v, grad_middle, sem()).start())
        outs.append(Copy(go_v, grad_out, sem()).start())
        for copy in later:
            copy.wait()
        prefix_back(q_v, go_v, at_v, to_v, c_v, t_v, gt_v)
        outs.append(Copy(c_v, centres, sem()).start())
        outs.append(Copy(gt_v, grad_table, sem()).start())
        for copy in outs:
            copy.wait()

    return kernel


def feed_back(layer, sec, g, slope, middle, mixed, attended, totals, table, packs, wo, we, wr):
    return call(
        feed_back_kernel(layer),
        (sec, g, slope, middle, mixed, attended, totals, table, *packs, *wo, *we, *wr),
        [SMEM] + [ANY] * 15,
        [
            ((LENGTH, WIDTH), F32), ((LENGTH, WIDTH), BF), ((HEADS, LENGTH), F32),
            ((PAD, 2 * WIDTH), F32),
        ],
        [
            vm((LENGTH, WIDTH)), vm((LENGTH, FF)), vm((LENGTH, WIDTH), F32), vm((LENGTH, WIDTH)),
            vm((LENGTH, WIDTH)), vm((HEADS, LENGTH), F32), vm((PAD, 2 * WIDTH)), vm((16, 1024), F32),
            vm((WIDTH, WIDTH)), vm((WIDTH, FF)), vm((FF, WIDTH)), vm((LENGTH, WIDTH), F32),
            vm((LENGTH, WIDTH)), vm((HEADS, LENGTH), F32), vm((PAD, 2 * WIDTH), F32), DMA((40,)),
        ],
        f"feed_back{layer}", 2 * LENGTH * WIDTH * 9 * WIDTH, 40 << 20,
    )


def attend_back_kernel():
    def kernel(
        sec, lens, mixed, grad_out, totals, centres, table, grad_mixed,
        m_v, go_v, to_v, c_v, t_v, gm_v, k_v, v_v, sems,
    ):
        sem = Sems(sems)
        pairs = ((mixed, m_v), (grad_out, go_v), (totals, to_v), (centres, c_v), (table, t_v))
        copies = [Copy(a, b, sem()).start() for a, b in pairs]
        for copy in copies:
            copy.wait()
        attend_back(m_v, go_v, to_v, c_v, t_v, lens, sec[0], gm_v, (k_v, v_v))
        Copy(gm_v, grad_mixed, sem()).start().wait()

    return kernel


def attend_backward(layer, sec, lens, mixed, grad_out, totals, centres, table):
    return call(
        attend_back_kernel(),
        (sec, lens, mixed, grad_out, totals, centres, table),
        [SMEM, SMEM] + [ANY] * 5,
        [((LENGTH, 3 * WIDTH), BF)],
        [
            vm((LENGTH, 3 * WIDTH)), vm((LENGTH, WIDTH)), vm((HEADS, LENGTH), F32),
            vm((HEADS, LENGTH), F32), vm((PAD, 2 * WIDTH)), vm((LENGTH, 3 * WIDTH)),
            vm((LENGTH, WIDTH), F32), vm((LENGTH, WIDTH), F32), DMA((8,)),
        ],
        f"attend_back{layer}", 2 * LENGTH * WIDTH * 10 * WIDTH, 16 << 20,
    )[0]


def mix_back_kernel(layer):
    def kernel(
        sec, grad_mixed, x, grad_middle, pack, pack2, w, w2, out,
        gm_v, x_v, mid_v, p_v, w_v, o_v, sems,
    ):
        own = sec[0] == layer
        sem = Sems(sems)
        source = x.at[sec[0]] if layer == 0 else x
        gms = [
            Copy(grad_mixed.at[tile(r, 256)], gm_v.at[tile(r, 256)], sem()).start()
            for r in range(1)
        ]
        ws = Copy(w, w_v, sem(), w2, own).start()
        gms += [
            Copy(grad_mixed.at[tile(r, 256)], gm_v.at[tile(r, 256)], sem()).start()
            for r in range(1, 4)
        ]
        packs = Copy(pack, p_v, sem(), pack2, own).start()
        xs = Copy(source, x_v, sem()).start()
        mids = Copy(grad_middle, mid_v, sem()).start()
        ws.wait()
        outs = []
        for r in range(4):
            rows = tile(r, 256)
            gms[r].wait()
            value = dot_nt(gm_v[rows], w_v[...])
            if r == 0:
                packs.wait()
                xs.wait()
                mids.wait()
            hat, scale = normalise(x_v[rows].astype(F32))
            value = mid_v[rows] + norm_back(value, p_v[GAIN_A : GAIN_A + 1], hat, scale)
            o_v[rows] = value.astype(BF)
            outs.append(Copy(o_v.at[rows], out.at[rows], sem()).start())
        for copy in outs:
            copy.wait()

    return kernel


def mix_back(layer, sec, grad_mixed, x, grad_middle, packs, weights):
    return call(
        mix_back_kernel(layer),
        (sec, grad_mixed, x, grad_middle, *packs, *weights),
        [SMEM] + [ANY] * 7,
        [((LENGTH, WIDTH), BF)],
        [
            vm((LENGTH, 3 * WIDTH)), vm((LENGTH, WIDTH)), vm((LENGTH, WIDTH), F32),
            vm((16, 1024), F32), vm((WIDTH, 3 * WIDTH)), vm((LENGTH, WIDTH)), DMA((16,)),
        ],
        f"mix_back{layer}", 2 * LENGTH * WIDTH * 3 * WIDTH, 20 << 20,
    )[0]


def prefix_kernel(count):
    def kernel(table, mine, weight, activity, embed, hidden, ge, gw, gb, gpw, gpb):
        total = jnp.zeros((PAD, activity.shape[1]), F32)
        for index in range(count):
            high, low = split(table[index])
            total = total + dot_nt(high, weight[index]) + dot_nt(low, weight[index])
        act = activity[...]
        pre = total * (1.0 - act * act)
        real = lax.broadcasted_iota(jnp.int32, pre.shape, 0) < PRE
        pre = jnp.where(real, pre, 0.0)
        high, low = split(pre)
        gb[...] = jnp.sum(pre, axis=0, keepdims=True)
        gw[...] = dot_tn(embed[...], high) + dot_tn(embed[...], low)
        ge[...] = dot_nt(high, hidden[...]) + dot_nt(low, hidden[...])
        part = mine[...]
        part = jnp.where(lax.broadcasted_iota(jnp.int32, part.shape, 0) < PRE, part, 0.0)
        high, low = split(part)
        rounded = act.astype(BF)
        gpw[...] = dot_tn(rounded, high) + dot_tn(rounded, low)
        gpb[...] = jnp.sum(part, axis=0, keepdims=True)

    return kernel


def prefix_grads(table, mine, weight, activity, embed, hidden):
    count, _, part = table.shape
    size = activity.shape[1]
    return call(
        prefix_kernel(count),
        (table, mine, weight, activity, embed, hidden),
        [VMEM] * 6,
        [
            ((PAD, WIDTH), F32), ((WIDTH, size), F32), ((1, size), F32), ((size, part), F32),
            ((1, part), F32),
        ],
        [],
        "prefix_grads", 1 << 30, 10 << 20,
        out_specs=[VMEM] * 5,
    )


def per_device(
    inputs, cotangent, doc_lengths, attend_gain, attend_bias, mixing_weight, mixing_bias,
    output_weight, output_bias, feed_gain, feed_bias, expand_weight, expand_bias, reduce_weight,
    reduce_bias, prefix_embed, hidden_weight, hidden_bias, prefix_weight, prefix_bias,
):
    section = lax.axis_index("section")
    sec = section.astype(jnp.int32).reshape(1)
    everyone = ("section", "dp")
    places = lax.axis_size("dp")
    swap = lambda value: lax.ppermute(value, "section", [(0, 1), (1, 0)])
    x = inputs.reshape(2, LENGTH, WIDTH)
    cot = cotangent.reshape(2, LENGTH, WIDTH)
    lens = doc_lengths.reshape(2, DOCS)

    wm = mixing_weight[0]
    wm2 = swap(wm)
    vectors = (
        attend_gain, attend_bias, mixing_bias, output_bias, feed_gain, feed_bias, expand_bias,
        reduce_bias,
    )
    pack = jnp.concatenate([v.astype(F32).reshape(-1, 1024) for v in vectors], 0)
    pack = jnp.pad(pack, ((0, 16 - pack.shape[0]), (0, 0)))
    pack2 = swap(pack)
    packs = (pack, pack2)

    activity = jnp.tanh(
        jnp.dot(prefix_embed, hidden_weight, preferred_element_type=F32) + hidden_bias
    )
    part = (
        jnp.dot(activity.astype(BF), prefix_weight[0], preferred_element_type=F32)
        + prefix_bias[0]
    ).astype(BF)
    part = jnp.pad(part, ((0, PAD - PRE), (0, 0))).astype(F32)
    tables = lax.all_to_all(
        jnp.broadcast_to(part[None], (2 * places, *part.shape)), everyone, 0, 0
    )
    tables = tables.reshape(2, places, PAD, -1).transpose(0, 2, 1, 3).reshape(2, PAD, 2 * WIDTH)
    tables = tables.astype(BF)
    full_prefix = lax.all_gather(prefix_weight[0], everyone, axis=0)

    wo, we = output_weight[0], expand_weight[0]
    wr = reduce_weight[0]
    wo_in, we_in, wm2 = lax.optimization_barrier((wo, we, wm2))
    wo2, we2 = swap(wo_in), swap(we_in)
    wms, wos, wes = (wm, wm2), (wo, wo2), (we, we2)

    kept = []
    hidden = x
    wrs = None
    for layer in range(2):
        mixed = mix(layer, sec, hidden, packs, wms)
        if wrs is None:
            wr_in, mixed = lax.optimization_barrier((wr, mixed))
            wrs = (wr, swap(wr_in))
        attended, totals, middle, slope, active = attend_expand(
            layer, sec, lens, hidden, mixed, tables[layer], packs, wos, wes
        )
        out = reduce(layer, sec, active, middle, packs, wrs)
        kept.append((hidden, mixed, attended, totals, middle, slope))
        hidden = out
        kept[-1] += (out,)
    out0, out1 = kept[0][-1], kept[1][-1]
    from_second = lax.ppermute(out0, "section", [(1, 0)])
    from_first = lax.ppermute(out1, "section", [(0, 1)])

    grad = cot
    grads, table_grads = [None, None], [None, None]
    for layer in (1, 0):
        before, mixed, attended, totals, middle, slope, _ = kept[layer]
        grad_middle, grad_out, centres, table_grads[layer] = feed_back(
            layer, sec, grad, slope, middle, mixed, attended, totals, tables[layer], packs,
            wos, wes, wrs,
        )
        grad_mixed = attend_backward(
            layer, sec, lens, mixed, grad_out, totals, centres, tables[layer]
        )
        grad = mix_back(layer, sec, grad_mixed, before, grad_middle, packs, wms)
        grads[layer] = grad
    grad_second = lax.ppermute(grads[0], "section", [(1, 0)])
    grad_first = lax.ppermute(grads[1], "section", [(0, 1)])

    def both(first, second, other_second, other_first):
        low = jnp.where(section == 0, first, other_first)
        high = jnp.where(section == 0, other_second, second)
        return jnp.stack([low, high])[None, :, None]

    layer_out = both(out0, out1, from_second, from_first)
    input_grad = both(grads[0], grads[1], grad_second, grad_first)

    send = jnp.stack(table_grads).reshape(2, PAD, places, -1).transpose(0, 2, 1, 3)
    send = send.reshape(2 * places, PAD, -1)
    mine = jnp.sum(lax.all_to_all(send, everyone, 0, 0), axis=0)
    summed = lax.all_to_all(
        jnp.broadcast_to(mine[None], (2 * places, *mine.shape)), everyone, 0, 0
    )
    pad_rows = ((0, PAD - PRE), (0, 0))
    ge, gw, gb, gpw, gpb = prefix_grads(
        summed, mine, full_prefix, jnp.pad(activity, pad_rows), jnp.pad(prefix_embed, pad_rows),
        hidden_weight,
    )
    return (layer_out, input_grad, ge[:PRE], gw, gb[0], gpw[None], gpb)


def solution(mesh):
    in_specs = (
        P(None, "dp", None, None),
        P(None, "dp", None, None),
        P(None, "dp", None),
        P("section", None),
        P("section", None),
        P("section", None, None),
        P("section", None),
        P("section", None, None),
        P("section", None),
        P("section", None),
        P("section", None),
        P("section", None, None),
        P("section", None),
        P("section", None, None),
        P("section", None),
        P(),
        P(),
        P(),
        P("section", None, "dp"),
        P("section", "dp"),
    )
    out_specs = (
        P("section", None, "dp", None, None),
        P("section", None, "dp", None, None),
        P(),
        P(),
        P(),
        P("section", None, "dp"),
        P("section", "dp"),
    )
    return jax.shard_map(
        per_device, mesh=mesh, in_specs=in_specs, out_specs=out_specs, check_vma=False
    )
```

```python
import jax
import jax.numpy as jnp
from jax import lax
from jax.experimental import pallas as pl
from jax.experimental.pallas import tpu as pltpu
from jax.sharding import PartitionSpec as P

F32 = jnp.float32
BF = jnp.bfloat16
LENGTH = 1024
WIDTH = 1024
FF = 4096
HEADS = 16
PRE = 10
PAD = 16
DOCS = 8
QB = 128
KC = 128
PAIRS = 8
STEPS = 5
NEG = -1e9
C0 = 0.7978845608028654
C1 = C0 * 0.044715

ANY = pl.BlockSpec(memory_space=pl.ANY)
SMEM = pl.BlockSpec(memory_space=pltpu.SMEM)
VMEM = pl.BlockSpec(memory_space=pltpu.VMEM)


def dot(a, b):
    return jnp.dot(a, b, preferred_element_type=F32)


def dot_nt(a, b):
    return lax.dot_general(a, b, (((1,), (1,)), ((), ())), preferred_element_type=F32)


def dot_tn(a, b):
    return lax.dot_general(a, b, (((0,), (0,)), ((), ())), preferred_element_type=F32)


def split(value):
    high = value.astype(BF)
    return high, (value - high.astype(F32)).astype(BF)


def call(kernel, ins, in_specs, outs, scratch, name, flops=0, moved=0, out_specs=None):
    return pl.pallas_call(
        kernel,
        in_specs=in_specs,
        out_specs=out_specs or [ANY] * len(outs),
        out_shape=[jax.ShapeDtypeStruct(s, d) for s, d in outs],
        scratch_shapes=scratch,
        compiler_params=pltpu.CompilerParams(vmem_limit_bytes=62 << 20),
        cost_estimate=pl.CostEstimate(flops=flops, bytes_accessed=moved, transcendentals=0),
        name=name,
    )(*ins)


class Copy:
    def __init__(self, source, target, sem, other=None, own=None):
        self.first = pltpu.make_async_copy(source, target, sem)
        self.second = None if other is None else pltpu.make_async_copy(other, target, sem)
        self.own = own

    def start(self):
        if self.second is None:
            self.first.start()
        else:
            pl.when(self.own)(self.first.start)
            pl.when(jnp.logical_not(self.own))(self.second.start)
        return self

    def wait(self):
        self.first.wait()


class Sems:
    def __init__(self, ref):
        self.ref = ref
        self.used = 0

    def __call__(self):
        self.used += 1
        return self.ref.at[self.used - 1]


GAIN_A, BIAS_A, BIAS_M, BIAS_O, GAIN_F, BIAS_F, BIAS_E, BIAS_R = 0, 1, 2, 5, 6, 7, 8, 12


def tile(index, rows):
    if isinstance(index, int):
        return slice(index * rows, (index + 1) * rows)
    return pl.ds(pl.multiple_of(index * rows, rows), rows)


def loop(count, body):
    def step(index, carry):
        body(index)
        return carry

    lax.fori_loop(0, count, step, 0)


def normalise(values):
    centre = jnp.mean(values, axis=-1, keepdims=True)
    shifted = values - centre
    variance = jnp.mean(shifted * shifted, axis=-1, keepdims=True)
    scale = lax.rsqrt(variance + 1e-5)
    return shifted * scale, scale


def norm_back(grad, gain, hat, scale):
    weighted = grad * gain
    first = jnp.mean(weighted, axis=-1, keepdims=True)
    second = jnp.mean(weighted * hat, axis=-1, keepdims=True)
    return scale * (weighted - first - hat * second)


def document_ends(lens, row):
    ends, total = [], None
    for doc in range(DOCS - 1):
        total = lens[row, doc] if total is None else total + lens[row, doc]
        ends.append(total)
    return ends


def window(ends, block):
    first = block * QB
    low = jnp.int32(0)
    for end in ends:
        low = jnp.maximum(low, jnp.where(first >= end, end, 0))
    count = (first + QB - low + KC - 1) // KC
    start = jnp.maximum(first + QB - count * KC, 0)
    return first, count, start


def visible(ends, first, start, count):
    places = first + lax.broadcasted_iota(jnp.int32, (1, QB), 1)
    low = jnp.zeros((1, QB), jnp.int32)
    for end in ends:
        low = jnp.maximum(low, jnp.where(places >= end, end, 0))
    keys = start + lax.broadcasted_iota(jnp.int32, (count * KC, QB), 0)
    inside = jnp.where((keys <= places) & (keys >= low), 0.0, NEG).astype(F32)
    prefix = lax.broadcasted_iota(jnp.int32, (PAD, QB), 0)
    prefix = jnp.where(prefix < PRE, 0.0, NEG).astype(F32)
    mask = jnp.concatenate([prefix, inside], 0)
    return jnp.concatenate([mask, mask], 1)


def spread(block):
    lane = lax.broadcasted_iota(jnp.int32, block.shape, 1) // 64
    zero = jnp.zeros_like(block)
    return jnp.concatenate([jnp.where(lane == h, block, zero) for h in range(2)], 0)


def gather_heads(block):
    both = [block[h * 64 : h * 64 + 64, h * QB : h * QB + QB] for h in range(2)]
    return jnp.concatenate(both, 0).T


def columns(pair, third):
    return slice(third * WIDTH + pair * 128, third * WIDTH + pair * 128 + 128)


def fold(op, parts):
    total = None
    for part in parts:
        for row in range(0, part.shape[0], 8):
            total = part[row : row + 8] if total is None else op(total, part[row : row + 8])
    return total


def pieces_of(size):
    return [slice(0, PAD)] + [slice(PAD + c, PAD + c + CUT) for c in range(0, size, CUT)]


CUT = 32


def attend_step(refs, ends, first, start, count, block):
    mixed, table, attended, totals = refs
    mask = visible(ends, first, start, count)
    rows = pl.ds(pl.multiple_of(first, QB), QB)
    keys = pl.ds(pl.multiple_of(start, QB), count * KC)
    lanes = pl.ds(pl.multiple_of(first, QB), QB)
    cuts = pieces_of(count * KC)

    def score(p):
        return dot_nt(
            jnp.concatenate([table[:, columns(p, 0)], mixed[keys, columns(p, 1)]], 0),
            spread(mixed[rows, columns(p, 0)]),
        )

    def soften(p, scores):
        parts = [scores[cut] + mask[cut] for cut in cuts]
        top = jnp.max(fold(jnp.maximum, parts), 0, keepdims=True)
        low, sums = [], None
        for part in parts:
            raised = jnp.exp(part - top)
            more = fold(jnp.add, [raised])
            sums = more if sums is None else sums + more
            low.append(raised.astype(BF))
        return jnp.concatenate(low, 0), jnp.sum(sums, 0, keepdims=True), top

    def combine(p, low):
        return dot_tn(
            jnp.concatenate([table[:, columns(p, 1)], mixed[keys, columns(p, 2)]], 0), low
        )

    def finish(p, out, total, top):
        log_total = top + jnp.log(total)
        for h in range(2):
            totals[pl.ds(2 * p + h, 1), lanes] = log_total[:, h * QB : h * QB + QB]
        attended[rows, columns(p, 0)] = gather_heads(out * (1.0 / total)).astype(BF)

    scores, soft, outs = {}, {}, {}
    for t in range(PAIRS + AHEAD + 2):
        if t < PAIRS:
            scores[t] = score(t)
        p = t - AHEAD
        if 0 <= p < PAIRS:
            soft[p] = soften(p, scores.pop(p))
            outs[p] = combine(p, soft[p][0])
        p -= 1
        if 0 <= p < PAIRS:
            finish(p, outs.pop(p), *soft.pop(p)[1:])


AHEAD = 3


def attend(mixed, table, lens, row, attended, totals):
    ends = document_ends(lens, row)

    def step(block, carry):
        first, count, start = window(ends, block)
        for size in range(1, STEPS + 1):

            @pl.when(count == size)
            def _():
                attend_step((mixed, table, attended, totals), ends, first, start, size, block)

        return carry

    lax.fori_loop(0, LENGTH // QB, step, 0)


def attend_back_step(refs, ends, first, start, count, block):
    mixed, grad_out, totals, centres, table, grad_mixed, key_sum, value_sum = refs
    mask = visible(ends, first, start, count)
    rows = pl.ds(pl.multiple_of(first, QB), QB)
    keys = pl.ds(pl.multiple_of(start, QB), count * KC)
    lanes = pl.ds(pl.multiple_of(first, QB), QB)
    def row_of(ref, p):
        return jnp.concatenate([ref[pl.ds(2 * p + h, 1), lanes] for h in range(2)], 1)

    cuts = pieces_of(count * KC)
    done = {}

    def products(p):
        query, grad = spread(mixed[rows, columns(p, 0)]), spread(grad_out[rows, columns(p, 0)])
        all_keys = jnp.concatenate([table[:, columns(p, 0)], mixed[keys, columns(p, 1)]], 0)
        all_values = jnp.concatenate([table[:, columns(p, 1)], mixed[keys, columns(p, 2)]], 0)
        return query, grad, all_keys, dot_nt(all_keys, query), dot_nt(all_values, grad)

    def soften(p, scores, grad_probs):
        total, centre = row_of(totals, p), row_of(centres, p)
        low, back = [], []
        for cut in cuts:
            probs = jnp.exp(scores[cut] + (mask[cut] - total))
            low.append(probs.astype(BF))
            back.append((probs * (grad_probs[cut] - centre)).astype(BF))
        return jnp.concatenate(low[1:], 0), jnp.concatenate(back, 0)

    def finish(p, query_grad, key_grad, value_grad):
        grad_mixed[rows, columns(p, 0)] = (gather_heads(query_grad) * 0.125).astype(BF)
        value_sum[keys, columns(p, 0)] += value_grad
        key_sum[keys, columns(p, 0)] += key_grad

    ready, grads = {}, {}
    for t in range(PAIRS + AHEAD_BACK + 2):
        if t < PAIRS:
            ready[t] = products(t)
        p = t - AHEAD_BACK
        if 0 <= p < PAIRS:
            query, grad, all_keys, scores, grad_probs = ready.pop(p)
            low, back = soften(p, scores, grad_probs)
            grads[p] = (dot_tn(all_keys, back), dot(back[PAD:], query), dot(low, grad))
        p -= 1
        if 0 <= p < PAIRS:
            finish(p, *grads.pop(p))


AHEAD_BACK = 2


def attend_back(mixed, grad_out, totals, centres, table, lens, row, grad_mixed, sums, arrive=None):
    ends = document_ends(lens, row)
    key_sum, value_sum = sums

    def clear(index, carry):
        rows = pl.ds(pl.multiple_of(index * 64, 64), 64)
        key_sum[rows, :] = jnp.zeros((64, WIDTH), F32)
        value_sum[rows, :] = jnp.zeros((64, WIDTH), F32)
        return carry

    lax.fori_loop(0, LENGTH // 64, clear, 0)

    def step(block, carry):
        first, count, start = window(ends, block)
        if arrive is not None:
            arrive(block)
        for size in range(1, STEPS + 1):

            @pl.when(count == size)
            def _():
                refs = (mixed, grad_out, totals, centres, table, grad_mixed, key_sum, value_sum)
                attend_back_step(refs, ends, first, start, size, block)

        return carry

    lax.fori_loop(0, LENGTH // QB, step, 0)

    def finish(index, carry):
        rows = pl.ds(pl.multiple_of(index * 64, 64), 64)
        grad_mixed[rows, WIDTH : 2 * WIDTH] = key_sum[rows, :].astype(BF)
        grad_mixed[rows, 2 * WIDTH :] = value_sum[rows, :].astype(BF)
        return carry

    lax.fori_loop(0, LENGTH // 64, finish, 0)


def prefix_back(queries, grad_out, attended, totals, centres, table, grad_table):
    heads = lax.broadcasted_iota(jnp.int32, (HEADS, WIDTH), 0)
    lanes = lax.broadcasted_iota(jnp.int32, (HEADS, WIDTH), 1)
    pick = jnp.where(lanes // 64 == heads, 1.0, 0.0).astype(BF)
    high, low = split(attended[...].astype(F32) * grad_out[...].astype(F32))
    centre = dot_nt(pick, high) + dot_nt(pick, low)
    centres[...] = centre
    real = lax.broadcasted_iota(jnp.int32, (4 * PAD, LENGTH), 0) % PAD < PRE
    lane = lax.broadcasted_iota(jnp.int32, (PAD, 256), 1) // 64

    def widen(block):
        zero = jnp.zeros_like(block)
        return jnp.concatenate([jnp.where(lane == h, block, zero) for h in range(4)], 0)

    def narrow(block):
        result = block[:PAD]
        for h in range(1, 4):
            result = jnp.where(lane == h, block[h * PAD : (h + 1) * PAD], result)
        return result

    def repeat(rows):
        return jnp.concatenate(
            [jnp.broadcast_to(rows[h : h + 1], (PAD, LENGTH)) for h in range(4)], 0
        )

    for quad in range(4):
        cols = slice(quad * 256, quad * 256 + 256)
        later = slice(WIDTH + quad * 256, WIDTH + quad * 256 + 256)
        mine = slice(quad * 4, quad * 4 + 4)
        scores = dot_nt(widen(table[:, cols]), queries[:, cols]) - repeat(totals[mine, :])
        probs = jnp.where(real, jnp.exp(scores), 0.0)
        grad_probs = dot_nt(widen(table[:, later]), grad_out[:, cols])
        grad_scores = (probs * (grad_probs - repeat(centre[mine, :]))).astype(BF)
        grad_table[:, cols] = narrow(dot(grad_scores, queries[:, cols]))
        grad_table[:, later] = narrow(dot(probs.astype(BF), grad_out[:, cols]))


def vm(shape, dtype=BF):
    return pltpu.VMEM(shape, dtype)


DMA = pltpu.SemaphoreType.DMA


def wait(copies):
    for copy in copies:
        copy.wait()


def rows_in(source, target, sem, count=4, start=True):
    size = source.shape[0] // count
    copies = [Copy(source.at[tile(r, size)], target.at[tile(r, size)], sem()) for r in range(count)]
    return [copy.start() for copy in copies] if start else copies


def rows_of(source, target, sem, count=4):
    size = source.shape[0] // count
    base = sem.used
    sem.used += count
    return lambda r: Copy(source.at[tile(r, size)], target.at[tile(r, size)], sem.ref.at[base + r])


def picked(pair, target, sem, own, cut=None, count=1):
    if cut is None:
        return [Copy(pair[0], target, sem(), pair[1], own)]
    size = target.shape[cut] // count
    index = [(tile(c, size),) if cut == 0 else (slice(None), tile(c, size)) for c in range(count)]
    return [Copy(pair[0].at[i], target.at[i], sem(), pair[1].at[i], own) for i in index]


def mix_phase(x_v, n_v, w_v, p_v, m_v, waits_x, waits_w, done):
    gain, bias = p_v[GAIN_A : GAIN_A + 1], p_v[BIAS_A : BIAS_A + 1]

    def norm(r):
        wait(waits_x[r] if waits_x else [])
        hat, _ = normalise(x_v[tile(r, 256)].astype(F32))
        n_v[tile(r, 256)] = (hat * gain + bias).astype(BF)

    norm(0)
    for j in range(3):
        wait(waits_w[j : j + 1])
        cols = tile(j, WIDTH)
        for r in range(4):
            value = dot(n_v[tile(r, 256)], w_v[:, cols]) + p_v[BIAS_M + j : BIAS_M + j + 1]
            value = value.astype(BF)
            if j == 0:
                value = value * jnp.asarray(0.125, BF)
                if r < 3:
                    norm(r + 1)
            m_v[tile(r, 256), cols] = value
        done(j)


def out_phase(x_v, at_v, wo_v, p_v, mid_v, n_v):
    gain, bias = p_v[GAIN_F : GAIN_F + 1], p_v[BIAS_F : BIAS_F + 1]
    for r in range(4):
        rows = tile(r, 256)
        value = x_v[rows].astype(F32) + dot(at_v[rows], wo_v[...]) + p_v[BIAS_O : BIAS_O + 1]
        mid_v[rows] = value
        hat, _ = normalise(value)
        n_v[rows] = (hat * gain + bias).astype(BF)


def gelu_both(value):
    square = value * value
    half = 0.5 * jnp.tanh(value * (C1 * square + C0)) + 0.5
    result = value * half
    return result, half + result * (1.0 - half) * ((6 * C1) * square + 2 * C0)


def expand_phase(n_v, we_v, p_v, a_v, s_v, rows, target, waits):
    for j in range(8):
        cols = tile(j, 512)
        part = tile(j % 2, 512)
        row = BIAS_E + j // 2
        wait(waits[j : j + 1])
        value = dot(n_v[rows], we_v[:, cols]) + p_v[row : row + 1, part]
        result, derivative = gelu_both(value)
        a_v[target, cols] = result.astype(BF)
        s_v[rows, cols] = derivative.astype(BF)


def reduce_phase(a_v, wr_v, p_v, mid_v, o_v, source, rows, waits):
    for n in range(4):
        cols = tile(n, 256)
        wait(waits[n : n + 1])
        value = dot(a_v[source], wr_v[:, cols]) + p_v[BIAS_R : BIAS_R + 1, cols]
        o_v[rows, cols] = (mid_v[rows, cols] + value).astype(BF)


def feed_back_phase(g_v, s_v, we_v, wr_v, wo_v, p_v, mid_v, go_v, waits, before):
    for r in range(2):
        rows = tile(r, 512)
        total = None
        for c in range(8):
            cols = tile(c, 512)
            if r == 0 and waits:
                wait(waits[c])
            value = dot_nt(g_v[rows], wr_v[cols]) * s_v[rows, cols].astype(F32)
            value = dot_nt(value.astype(BF), we_v[:, cols])
            total = value if total is None else total + value
        if r == 0:
            wait(before)
        gain = p_v[GAIN_F : GAIN_F + 1]
        for half in range(2):
            rows = tile(2 * r + half, 256)
            hat, scale = normalise(mid_v[rows])
            value = norm_back(total[tile(half, 256)], gain, hat, scale)
            value = g_v[rows].astype(F32) + value
            mid_v[rows] = value
            go_v[rows] = dot_nt(value.astype(BF), wo_v[...]).astype(BF)


def mix_back_phase(gm_v, w_v, x_v, mid_v, p_v, o_v, waits, done):
    def step(r):
        rows = tile(r, 256)
        waits(r)
        value = dot_nt(gm_v[rows], w_v[...])
        hat, scale = normalise(x_v[rows].astype(F32))
        value = mid_v[rows] + norm_back(value, p_v[GAIN_A : GAIN_A + 1], hat, scale)
        o_v[rows] = value.astype(BF)
        done(r)

    loop(4, step)


def join_table(pieces, t_v):
    size = pieces.shape[2]
    for index in range(pieces.shape[0]):
        t_v[:, tile(index, size)] = pieces[index].astype(BF)


def cut_table(table, pieces):
    size = pieces.shape[2]
    for index in range(pieces.shape[0]):
        pieces[index] = table[:, tile(index, size)]


def prologue_kernel(
    embed, hidden_weight, hidden_bias, weight, bias, ga, ba, bm, bo, gf, bf, be, br,
    pack, activity, wide, part, e_v,
):
    pack[...] = jnp.zeros(pack.shape, F32)
    row = 0
    for ref in (ga, ba, bm, bo, gf, bf, be, br):
        for index in range(ref.shape[1] // 1024):
            pack[row : row + 1] = ref[:, tile(index, 1024)].astype(F32)
            row += 1
    e_v[...] = jnp.zeros(e_v.shape, F32)
    e_v[:PRE] = embed[...].astype(F32)
    rounded = e_v[...].astype(BF)
    wide[...] = rounded
    act = jnp.tanh(dot(rounded, hidden_weight[...]) + hidden_bias[...].astype(F32)[None])
    activity[...] = act
    value = dot(act.astype(BF), weight[...]) + bias[...].astype(F32)
    part[...] = jnp.broadcast_to(value.astype(BF)[None], part.shape)


def begin(copies):
    return [copy.start() for copy in copies]


def mix_attend_kernel(
    sec, lens, x, table, pack, pack2, w, w2, mixed, attended, totals,
    x_v, n_v, w_v, p_v, m_v, tp_v, t_v, at_v, to_v, sems,
):
    own = sec[0] == 0
    sem = Sems(sems)
    packs = picked((pack, pack2), p_v, sem, own)
    xs = rows_in(x.at[sec[0]], x_v, sem, start=False)
    ws = picked((w, w2), w_v, sem, own, 1, 3)
    tabs = [Copy(table, tp_v, sem())]
    begin(packs)
    begin(xs[:1])
    begin(ws[:1])
    wait(packs)
    wait(xs[:1])
    begin(xs[1:])
    begin(ws[1:])
    begin(tabs)
    outs = []

    def done(j):
        cols = tile(j, WIDTH)
        outs.append(Copy(m_v.at[:, cols], mixed.at[:, cols], sem()).start())

    mix_phase(x_v, n_v, w_v, p_v, m_v, [[]] + [xs[r : r + 1] for r in range(1, 4)], ws, done)
    wait(tabs)
    join_table(tp_v, t_v)
    attend(m_v, t_v, lens, sec[0], at_v, to_v)
    outs += [Copy(at_v, attended, sem()).start(), Copy(to_v, totals, sem()).start()]
    wait(outs)


def mix_attend(sec, lens, x, table, packs, weights):
    return call(
        mix_attend_kernel,
        (sec, lens, x, table, *packs, *weights),
        [SMEM, SMEM] + [ANY] * 6,
        [((LENGTH, 3 * WIDTH), BF), ((LENGTH, WIDTH), BF), ((HEADS, LENGTH), F32)],
        [
            vm((LENGTH, WIDTH)), vm((LENGTH, WIDTH)), vm((WIDTH, 3 * WIDTH)), vm((16, 1024), F32),
            vm((LENGTH, 3 * WIDTH)), vm(table.shape, table.dtype), vm((PAD, 2 * WIDTH)),
            vm((LENGTH, WIDTH)), vm((HEADS, LENGTH), F32), DMA((16,)),
        ],
        "mix_attend", 2 * LENGTH * WIDTH * 6 * WIDTH, 20 << 20,
    )


def middle_kernel(
    sec, lens, x, attended, table, cot, pack, pack2, wm, wm2, wo, wo2, we, we2, wr, wr2,
    keep, send, grad_in, middle, slope, grad_table,
    p0_v, p_v, x_v, n_v, g_v, at_v, wm_v, wo_v, m_v, mid_v, to_v, tp_v, t_v, c_v, gt_v, sems,
):
    own0, own = sec[0] == 0, sec[0] == 1
    sem = Sems(sems)
    packs = picked((pack, pack2), p0_v, sem, own0) + picked((pack, pack2), p_v, sem, own)
    wms = picked((wm, wm2), wm_v, sem, own, 1, 3)
    wos0 = picked((wo, wo2), wo_v, sem, own0)
    wos = picked((wo, wo2), wo_v, sem, own)
    tabs = [Copy(table, tp_v, sem())]
    cots = [Copy(cot.at[sec[0]], g_v, sem())]
    grads = rows_of(g_v, grad_in, sem)
    mids = [Copy(mid_v, middle, sem())]
    xs = [Copy(x.at[sec[0]], n_v, sem()), Copy(attended, at_v, sem())]

    def chosen(source, first):
        ends = (keep, send) if first else (send, keep)
        base = sem.used
        sem.used += 4

        def copy(r):
            rows = tile(r, 256)
            choice = [pltpu.make_async_copy(source.at[rows], end.at[rows], sems.at[base + r]) for end in ends]

            class Out:
                def start(self):
                    pl.when(own0)(choice[0].start)
                    pl.when(own)(choice[1].start)

                def wait(self):
                    choice[0].wait()

            return Out()

        return [copy(r) for r in range(4)]

    out0s, out1s = chosen(x_v, True), chosen(n_v, False)

    def first_scope(wr_v, we_v, s_v, a_v):
        wes = picked((we, we2), we_v, sem, own0, 1, 8)
        wrs = picked((wr, wr2), wr_v, sem, own0, 1, 4)
        begin(wos0)
        begin(xs)
        begin(packs)
        wait(wos0)
        wait(xs)
        begin(wes)
        begin(wrs)
        wait(packs)
        out_phase(n_v, at_v, wo_v, p0_v, mid_v, n_v)
        begin(mids)
        begin(wos)
        begin(wms)
        begin(tabs)
        begin(cots)
        slopes = rows_in(s_v, slope, sem, start=False)
        for r in range(4):
            rows = tile(r, 256)
            expand_phase(n_v, we_v, p0_v, a_v, s_v, rows, slice(0, 256), wes if r == 0 else [])
            slopes[r].start()
            reduce_phase(
                a_v, wr_v, p0_v, mid_v, x_v, slice(0, 256), rows, wrs if r == 0 else []
            )
            out0s[r].start()
        wait(slopes)

    pl.run_scoped(first_scope, vm((FF, WIDTH)), vm((WIDTH, FF)), vm((LENGTH, FF)), vm((256, FF)))

    def feed_scope(wr_v, we_v, s_v, a_v):
        wes = picked((we, we2), we_v, sem, own, 1, 8)
        wrs = picked((wr, wr2), wr_v, sem, own, 0, 2)
        begin(wes)
        begin(wrs)
        mix_phase(x_v, n_v, wm_v, p_v, m_v, [], wms, lambda j: None)
        wait(tabs)
        join_table(tp_v, t_v)
        attend(m_v, t_v, lens, sec[0], at_v, to_v)
        wait(wos)
        wait(mids)
        out_phase(x_v, at_v, wo_v, p_v, mid_v, n_v)
        for r in range(4):
            rows = tile(r, 256)
            expand_phase(n_v, we_v, p_v, a_v, s_v, rows, slice(0, 256), wes if r == 0 else [])
            if r == 0:
                wait(wrs)
            reduce_phase(a_v, wr_v, p_v, mid_v, n_v, slice(0, 256), rows, [])
            out1s[r].start()
        wait(cots)
        feed_back_phase(g_v, s_v, we_v, wr_v, wo_v, p_v, mid_v, n_v, [], out1s)

    pl.run_scoped(feed_scope, vm((FF, WIDTH)), vm((WIDTH, FF)), vm((LENGTH, FF)), vm((256, FF)))

    prefix_back(m_v, n_v, at_v, to_v, c_v, t_v, gt_v)
    table_out = Copy(gt_v, grad_table, sem()).start()

    def attend_scope(gm_v, k_v, v_v):
        attend_back(m_v, n_v, to_v, c_v, t_v, lens, sec[0], gm_v, (k_v, v_v))
        mix_back_phase(
            gm_v, wm_v, x_v, mid_v, p_v, g_v, lambda r: None, lambda r: grads(r).start()
        )

    pl.run_scoped(
        attend_scope, vm((LENGTH, 3 * WIDTH)), vm((LENGTH, WIDTH), F32), vm((LENGTH, WIDTH), F32)
    )

    wait(out0s)
    table_out.wait()
    wait([grads(r) for r in range(4)])


def pack_payload(tables, weight, out):
    pieces, size, part = weight.shape
    each = pieces // 2
    total = jnp.zeros((2 * PAD, size), F32)
    for layer, table in enumerate(tables):
        for index in range(each):
            cols = tile(index, part)
            both = jnp.concatenate(split(table[:, cols]), 0)
            total = total + dot_nt(both, weight[layer * each + index])
            if out.dtype == BF:
                out[layer * each + index, : 2 * PAD] = both
    share = total[:PAD] + total[PAD:]
    if out.dtype == BF:
        rows = [share[:, tile(k, 128)] for k in range(size // 128)]
        shared = jnp.concatenate(rows, 0).astype(BF)
        for index in range(pieces):
            out[index, 2 * PAD :] = shared
    else:
        for layer, table in enumerate(tables):
            out[layer * PAD : (layer + 1) * PAD] = table[...]
        out[2 * PAD :, :size] = share


def middle_part(sec, lens, x, attended, table, cot, packs, wm, wo, we, wr):
    return call(
        middle_kernel,
        (sec, lens, x, attended, table, cot, *packs, *wm, *wo, *we, *wr),
        [SMEM, SMEM] + [ANY] * 14,
        [
            ((LENGTH, WIDTH), BF), ((LENGTH, WIDTH), BF), ((LENGTH, WIDTH), BF),
            ((LENGTH, WIDTH), F32), ((LENGTH, FF), BF), ((PAD, 2 * WIDTH), F32),
        ],
        [
            vm((16, 1024), F32), vm((16, 1024), F32), vm((LENGTH, WIDTH)), vm((LENGTH, WIDTH)),
            vm((LENGTH, WIDTH)), vm((LENGTH, WIDTH)), vm((WIDTH, 3 * WIDTH)), vm((WIDTH, WIDTH)),
            vm((LENGTH, 3 * WIDTH)), vm((LENGTH, WIDTH), F32), vm((HEADS, LENGTH), F32),
            vm(table.shape, table.dtype), vm((PAD, 2 * WIDTH)), vm((HEADS, LENGTH), F32),
            vm((PAD, 2 * WIDTH), F32), DMA((80,)),
        ],
        "middle", 2 * LENGTH * WIDTH * 36 * WIDTH, 80 << 20,
    )


def feed_back_kernel(
    sec, g, slope, middle, mixed, attended, totals, table, other, weight, pack, pack2, wo, wo2,
    we, we2, wr, wr2,
    grad_middle, grad_out, centres, payload,
    g_v, s_v, mid_v, q_v, at_v, to_v, tp_v, t_v, p_v, wo_v, we_v, wr_v, go_v, c_v, gt_v, gt0_v,
    pw_v, pay_v, sems,
):
    own = sec[0] == 0
    sem = Sems(sems)
    gs = rows_in(g, g_v, sem, 2, start=False)
    wrs = picked((wr, wr2), wr_v, sem, own, 0, 8)
    wes = picked((we, we2), we_v, sem, own, 1, 8)
    begin(gs[:1])
    parts = []
    for c in range(8):
        cols = tile(c, 512)
        parts.append([wrs[c], Copy(slope.at[:, cols], s_v.at[:, cols], sem()), wes[c]])
    begin(parts[0])
    wait(gs[:1])
    for c in range(1, 8):
        begin(parts[c])
    before = [
        gs[1].start(),
        picked((pack, pack2), p_v, sem, own)[0].start(),
        Copy(middle, mid_v, sem()).start(),
        picked((wo, wo2), wo_v, sem, own)[0].start(),
    ]
    later = [
        Copy(mixed.at[:, :WIDTH], q_v, sem()).start(),
        Copy(attended, at_v, sem()).start(),
        Copy(totals, to_v, sem()).start(),
        Copy(table, tp_v, sem()).start(),
        Copy(other, gt_v, sem()).start(),
        Copy(weight, pw_v, sem()).start(),
    ]
    feed_back_phase(g_v, s_v, we_v, wr_v, wo_v, p_v, mid_v, go_v, parts, before)
    outs = [Copy(mid_v, grad_middle, sem()).start(), Copy(go_v, grad_out, sem()).start()]
    wait(later)
    join_table(tp_v, t_v)
    prefix_back(q_v, go_v, at_v, to_v, c_v, t_v, gt0_v)
    outs.append(Copy(c_v, centres, sem()).start())
    pack_payload((gt0_v, gt_v), pw_v, pay_v)
    outs.append(Copy(pay_v, payload, sem()).start())
    wait(outs)


def feed_back(sec, g, slope, middle, mixed, attended, totals, table, other, weight, packs, wo, we, wr):
    size = weight.shape[1]
    if weight.shape[2] == 128:
        payload = ((weight.shape[0], 2 * PAD + PAD * size // 128, 128), BF)
    else:
        payload = ((3 * PAD, 2 * WIDTH), F32)
    return call(
        feed_back_kernel,
        (
            sec, g, slope, middle, mixed, attended, totals, table, other, weight, *packs, *wo,
            *we, *wr,
        ),
        [SMEM] + [ANY] * 17,
        [((LENGTH, WIDTH), F32), ((LENGTH, WIDTH), BF), ((HEADS, LENGTH), F32), payload],
        [
            vm((LENGTH, WIDTH)), vm((LENGTH, FF)), vm((LENGTH, WIDTH), F32), vm((LENGTH, WIDTH)),
            vm((LENGTH, WIDTH)), vm((HEADS, LENGTH), F32), vm(table.shape, table.dtype),
            vm((PAD, 2 * WIDTH)), vm((16, 1024), F32),
            vm((WIDTH, WIDTH)), vm((WIDTH, FF)), vm((FF, WIDTH)),
            vm((LENGTH, WIDTH)), vm((HEADS, LENGTH), F32), vm((PAD, 2 * WIDTH), F32),
            vm((PAD, 2 * WIDTH), F32), vm(weight.shape), vm(*payload), DMA((48,)),
        ],
        "feed_back", 2 * LENGTH * WIDTH * 9 * WIDTH, 40 << 20,
    )


def last_kernel(
    sec, lens, mixed, grad_out, totals, centres, table, x, grad_middle, grad1, keep, other,
    pack, pack2, w, w2,
    layer_out, input_grad, send,
    m_v, go_v, to_v, c_v, tp_v, t_v, gm_v, k_v, v_v, b_v, x_v, mid_v, p_v, w_v, o_v, sems,
):
    own = sec[0] == 0
    sem = Sems(sems)
    pairs = ((table, tp_v), (totals, to_v), (centres, c_v))
    copies = [Copy(a, b, sem()).start() for a, b in pairs]
    blocks = LENGTH // QB
    queries = rows_of(mixed, m_v, sem, blocks)
    outs_in = rows_of(grad_out, go_v, sem, blocks)
    for block in range(blocks):
        queries(block).start()
        outs_in(block).start()
    later = picked((pack, pack2), p_v, sem, own) + picked((w, w2), w_v, sem, own)
    later += [Copy(x.at[sec[0]], x_v, sem()), Copy(grad_middle, mid_v, sem())]
    ins = [
        Copy(keep, b_v.at[0], sem()), Copy(other, b_v.at[1], sem()), Copy(grad1, b_v.at[2], sem())
    ]
    outs = [
        Copy(b_v.at[0], layer_out.at[sec[0]], sem()),
        Copy(b_v.at[1], layer_out.at[1 - sec[0]], sem()),
    ]
    grad1_sem, base = sem(), sem.used
    grad1_outs = [
        pltpu.make_async_copy(b_v.at[2], target, grad1_sem) for target in (send, input_grad.at[1])
    ]
    wait(copies)
    join_table(tp_v, t_v)

    def arrive(block):
        queries(block).wait()
        outs_in(block).wait()

        @pl.when(block == 1)
        def _():
            begin(later)

        @pl.when(block == 3)
        def _():
            begin(ins)

        @pl.when(block == 5)
        def _():
            wait(ins)
            begin(outs)
            pl.when(own)(grad1_outs[0].start)
            pl.when(jnp.logical_not(own))(grad1_outs[1].start)

    attend_back(m_v, go_v, to_v, c_v, t_v, lens, sec[0], gm_v, (k_v, v_v), arrive)
    wait(later)

    def grad0(r):
        rows = tile(r, 256)
        return [
            pltpu.make_async_copy(o_v.at[rows], target.at[rows], sems.at[base + r])
            for target in (input_grad.at[0], send)
        ]

    def done(r):
        pl.when(own)(grad0(r)[0].start)
        pl.when(jnp.logical_not(own))(grad0(r)[1].start)

    mix_back_phase(gm_v, w_v, x_v, mid_v, p_v, o_v, lambda r: None, done)
    wait(outs)
    grad1_outs[0].wait()
    for r in range(4):
        grad0(r)[0].wait()


def last_part(sec, lens, mixed, grad_out, totals, centres, table, x, grad_middle, outs, packs, wm):
    return call(
        last_kernel,
        (sec, lens, mixed, grad_out, totals, centres, table, x, grad_middle, *outs, *packs, *wm),
        [SMEM, SMEM] + [ANY] * 14,
        [((2, LENGTH, WIDTH), BF), ((2, LENGTH, WIDTH), BF), ((LENGTH, WIDTH), BF)],
        [
            vm((LENGTH, 3 * WIDTH)), vm((LENGTH, WIDTH)), vm((HEADS, LENGTH), F32),
            vm((HEADS, LENGTH), F32), vm(table.shape, table.dtype), vm((PAD, 2 * WIDTH)),
            vm((LENGTH, 3 * WIDTH)), vm((LENGTH, WIDTH), F32), vm((LENGTH, WIDTH), F32),
            vm((3, LENGTH, WIDTH)), vm((LENGTH, WIDTH)), vm((LENGTH, WIDTH), F32),
            vm((16, 1024), F32), vm((WIDTH, 3 * WIDTH)), vm((LENGTH, WIDTH)), DMA((48,)),
        ],
        "last", 2 * LENGTH * WIDTH * 13 * WIDTH, 50 << 20,
    )


def place_kernel(sec, other, grads, out, b_v, sems):
    parts = rows_in(other, b_v, Sems(sems.at[pl.ds(0, 4)]), start=False)
    target = out.at[1 - sec[0]]
    outs = rows_in(b_v, target, Sems(sems.at[pl.ds(4, 4)]), start=False)
    begin(parts)
    for r in range(4):
        parts[r].wait()
        outs[r].start()
    wait(outs)


def place(sec, other, grads):
    return pl.pallas_call(
        place_kernel,
        in_specs=[SMEM, ANY, ANY],
        out_specs=ANY,
        out_shape=jax.ShapeDtypeStruct(grads.shape, grads.dtype),
        scratch_shapes=[vm((LENGTH, WIDTH)), DMA((8,))],
        input_output_aliases={2: 0},
        compiler_params=pltpu.CompilerParams(vmem_limit_bytes=62 << 20),
        cost_estimate=pl.CostEstimate(flops=0, bytes_accessed=4 << 20, transcendentals=0),
        name="place",
    )(sec, other, grads)


def prefix_kernel(parts, activity, embed, hidden, ge, gw, gb, gpw, gpb):
    total = parts[0].astype(F32)
    for index in range(1, parts.shape[0]):
        total = total + parts[index].astype(F32)
    act = activity[...]
    share = [total[(2 + k) * PAD : (3 + k) * PAD] for k in range(act.shape[1] // 128)]
    pre = jnp.concatenate(share, 1) * (1.0 - act * act)
    pre = jnp.where(lax.broadcasted_iota(jnp.int32, pre.shape, 0) < PRE, pre, 0.0)
    high, low = split(pre)
    gb[...] = jnp.sum(pre, axis=0, keepdims=True)
    gw[...] = dot_tn(embed[...], high) + dot_tn(embed[...], low)
    ge[...] = dot_nt(high, hidden[...]) + dot_nt(low, hidden[...])
    mine = total[:PAD] + total[PAD : 2 * PAD]
    mine = jnp.where(lax.broadcasted_iota(jnp.int32, mine.shape, 0) < PRE, mine, 0.0)
    high, low = split(mine)
    rounded = act.astype(BF)
    size = gpw.shape[1]
    gpw[...] = (dot_tn(rounded, high) + dot_tn(rounded, low))[:, :size]
    gpb[...] = jnp.sum(mine, axis=0, keepdims=True)[:, :size]


def prefix_grads(parts, activity, embed, hidden, share):
    size = activity.shape[1]
    return call(
        prefix_kernel,
        (parts, activity, embed, hidden),
        [VMEM] * 4,
        [
            ((PAD, WIDTH), F32), ((WIDTH, size), F32), ((1, size), F32), ((size, share), F32),
            ((1, share), F32),
        ],
        [],
        "prefix_grads", 1 << 30, 10 << 20,
        out_specs=[VMEM] * 5,
    )


def per_device(
    inputs, cotangent, doc_lengths, attend_gain, attend_bias, mixing_weight, mixing_bias,
    output_weight, output_bias, feed_gain, feed_bias, expand_weight, expand_bias, reduce_weight,
    reduce_bias, prefix_embed, hidden_weight, hidden_bias, prefix_weight, prefix_bias,
):
    section = lax.axis_index("section")
    sec = section.astype(jnp.int32).reshape(1)
    everyone = ("section", "dp")
    places = lax.axis_size("dp")
    swap = lambda value: lax.ppermute(value, "section", [(0, 1), (1, 0)])
    x = inputs.reshape(2, LENGTH, WIDTH)
    cot = cotangent.reshape(2, LENGTH, WIDTH)
    lens = doc_lengths.reshape(2, DOCS)
    share = prefix_weight.shape[2]

    wm, wo, we, wr = mixing_weight[0], output_weight[0], expand_weight[0], reduce_weight[0]
    wm2 = swap(wm)
    vectors = (
        attend_gain, attend_bias, mixing_bias, output_bias, feed_gain, feed_bias, expand_bias,
        reduce_bias,
    )
    pack, activity, embed, part = call(
        prologue_kernel,
        (prefix_embed, hidden_weight, hidden_bias, prefix_weight[0], prefix_bias, *vectors),
        [VMEM] * 13,
        [
            ((16, 1024), F32), ((PAD, hidden_weight.shape[1]), F32), ((PAD, WIDTH), BF),
            ((2 * places, PAD, share), BF),
        ],
        [vm((PAD, WIDTH), F32)],
        "prologue", 1 << 24, 2 << 20,
        out_specs=[VMEM] * 4,
    )
    pack2 = swap(pack)

    tables = lax.all_to_all(part, everyone, 0, 0)
    tables = tables.reshape(2, places, PAD, share)
    if share % 128:
        tables = tables.transpose(0, 2, 1, 3).reshape(2, 1, PAD, 2 * WIDTH)
    full = lax.all_gather(prefix_weight[0], everyone, axis=0)
    if share != 128:
        full = full.reshape(2, places, -1, share).transpose(0, 2, 1, 3)
        full = full.reshape(2, -1, 2 * WIDTH)
    wm2, pack2, tables = lax.optimization_barrier((wm2, pack2, tables))
    packs = (pack, pack2)

    wo_in, we_in, wr_in, wm2 = lax.optimization_barrier((wo, we, wr, wm2))
    wo2, we2, wr2 = swap(wo_in), swap(we_in), swap(wr_in)
    wms, wos, wes, wrs = (wm, wm2), (wo, wo2), (we, we2), (wr, wr2)

    mixed, attended, totals = mix_attend(sec, lens, x, tables[0], packs, wms)
    keep, send, grad1, middle, slope, table_grad1 = middle_part(
        sec, lens, x, attended, tables[1], cot, packs, wms, wos, wes, wrs
    )
    other = swap(send)
    grad_middle, grad_out, centres, payload = feed_back(
        sec, grad1, slope, middle, mixed, attended, totals, tables[0], table_grad1, full, packs,
        wos, wes, wrs,
    )

    if share != 128:
        table_grads = jnp.stack(split(payload[: 2 * PAD].reshape(2, PAD, places, share)), 0)
        table_grads = table_grads.transpose(1, 3, 0, 2, 4).reshape(2 * places, 2 * PAD, share)
        table_grads = jnp.pad(table_grads, ((0, 0), (0, 0), (0, 128 - share)))
        units = payload[2 * PAD :, : activity.shape[1]].reshape(PAD, -1, 128).transpose(1, 0, 2)
        units = jnp.broadcast_to(units.astype(BF).reshape(1, -1, 128), (2 * places, units.size // 128, 128))
        payload = jnp.concatenate([table_grads, units], 1)
    parts = lax.all_to_all(payload, everyone, 0, 0)
    layer_out, grads, send = last_part(
        sec, lens, mixed, grad_out, totals, centres, tables[0], x, grad_middle,
        (grad1, keep, other), packs, wms,
    )
    parts, send, grads = lax.optimization_barrier((parts, send, grads))
    other = swap(send)
    ge, gw, gb, gpw, gpb = prefix_grads(parts, activity, embed, hidden_weight, share)
    input_grad = place(sec, other, grads)
    shape = (1, 2, 1, LENGTH, WIDTH)
    return (
        layer_out.reshape(shape), input_grad.reshape(shape), ge[:PRE], gw, gb[0], gpw[None], gpb
    )


def solution(mesh):
    in_specs = (
        P(None, "dp", None, None),
        P(None, "dp", None, None),
        P(None, "dp", None),
        P("section", None),
        P("section", None),
        P("section", None, None),
        P("section", None),
        P("section", None, None),
        P("section", None),
        P("section", None),
        P("section", None),
        P("section", None, None),
        P("section", None),
        P("section", None, None),
        P("section", None),
        P(),
        P(),
        P(),
        P("section", None, "dp"),
        P("section", "dp"),
    )
    out_specs = (
        P("section", None, "dp", None, None),
        P("section", None, "dp", None, None),
        P(),
        P(),
        P(),
        P("section", None, "dp"),
        P("section", "dp"),
    )
    return jax.shard_map(
        per_device, mesh=mesh, in_specs=in_specs, out_specs=out_specs, check_vma=False
    )
```

```python
import jax
import jax.numpy as jnp
from jax import lax
from jax.experimental import pallas as pl
from jax.experimental.pallas import tpu as pltpu
from jax.sharding import PartitionSpec as P

F32 = jnp.float32
BF = jnp.bfloat16
LENGTH = 1024
WIDTH = 1024
FF = 4096
HEADS = 16
PRE = 10
PAD = 16
DOCS = 8
QB = 128
KC = 128
PAIRS = 8
STEPS = 5
NEG = -1e9
C0 = 0.7978845608028654
C1 = C0 * 0.044715

ANY = pl.BlockSpec(memory_space=pl.ANY)
SMEM = pl.BlockSpec(memory_space=pltpu.SMEM)
VMEM = pl.BlockSpec(memory_space=pltpu.VMEM)


def dot(a, b):
    return jnp.dot(a, b, preferred_element_type=F32)


def dot_nt(a, b):
    return lax.dot_general(a, b, (((1,), (1,)), ((), ())), preferred_element_type=F32)


def dot_tn(a, b):
    return lax.dot_general(a, b, (((0,), (0,)), ((), ())), preferred_element_type=F32)


def split(value):
    high = value.astype(BF)
    return high, (value - high.astype(F32)).astype(BF)


def call(kernel, ins, in_specs, outs, scratch, name, flops=0, moved=0, out_specs=None):
    return pl.pallas_call(
        kernel,
        in_specs=in_specs,
        out_specs=out_specs or [ANY] * len(outs),
        out_shape=[jax.ShapeDtypeStruct(s, d) for s, d in outs],
        scratch_shapes=scratch,
        compiler_params=pltpu.CompilerParams(vmem_limit_bytes=62 << 20),
        cost_estimate=pl.CostEstimate(flops=flops, bytes_accessed=moved, transcendentals=0),
        name=name,
    )(*ins)


class Copy:
    def __init__(self, source, target, sem, other=None, own=None):
        self.first = pltpu.make_async_copy(source, target, sem)
        self.second = None if other is None else pltpu.make_async_copy(other, target, sem)
        self.own = own

    def start(self):
        if self.second is None:
            self.first.start()
        else:
            pl.when(self.own)(self.first.start)
            pl.when(jnp.logical_not(self.own))(self.second.start)
        return self

    def wait(self):
        self.first.wait()


class Sems:
    def __init__(self, ref):
        self.ref = ref
        self.used = 0

    def __call__(self):
        self.used += 1
        return self.ref.at[self.used - 1]


GAIN_A, BIAS_A, BIAS_M, BIAS_O, GAIN_F, BIAS_F, BIAS_E, BIAS_R = 0, 1, 2, 5, 6, 7, 8, 12


def tile(index, rows):
    if isinstance(index, int):
        return slice(index * rows, (index + 1) * rows)
    return pl.ds(pl.multiple_of(index * rows, rows), rows)


def loop(count, body):
    def step(index, carry):
        body(index)
        return carry

    lax.fori_loop(0, count, step, 0)


def normalise(values):
    centre = jnp.mean(values, axis=-1, keepdims=True)
    shifted = values - centre
    variance = jnp.mean(shifted * shifted, axis=-1, keepdims=True)
    scale = lax.rsqrt(variance + 1e-5)
    return shifted * scale, scale


def norm_back(grad, gain, hat, scale):
    weighted = grad * gain
    first = jnp.mean(weighted, axis=-1, keepdims=True)
    second = jnp.mean(weighted * hat, axis=-1, keepdims=True)
    return scale * (weighted - first - hat * second)


def document_ends(lens, row):
    ends, total = [], None
    for doc in range(DOCS - 1):
        total = lens[row, doc] if total is None else total + lens[row, doc]
        ends.append(total)
    return ends


def window(ends, block):
    first = block * QB
    low = jnp.int32(0)
    for end in ends:
        low = jnp.maximum(low, jnp.where(first >= end, end, 0))
    count = (first + QB - low + KC - 1) // KC
    start = jnp.maximum(first + QB - count * KC, 0)
    return first, count, start


def visible(ends, first, start, count):
    places = first + lax.broadcasted_iota(jnp.int32, (1, QB), 1)
    low = jnp.zeros((1, QB), jnp.int32)
    for end in ends:
        low = jnp.maximum(low, jnp.where(places >= end, end, 0))
    keys = start + lax.broadcasted_iota(jnp.int32, (count * KC, QB), 0)
    inside = jnp.where((keys <= places) & (keys >= low), 0.0, NEG).astype(F32)
    prefix = lax.broadcasted_iota(jnp.int32, (PAD, QB), 0)
    prefix = jnp.where(prefix < PRE, 0.0, NEG).astype(F32)
    mask = jnp.concatenate([prefix, inside], 0)
    return jnp.concatenate([mask, mask], 1)


def spread(block):
    lane = lax.broadcasted_iota(jnp.int32, block.shape, 1) // 64
    zero = jnp.zeros_like(block)
    return jnp.concatenate([jnp.where(lane == h, block, zero) for h in range(2)], 0)


def gather_heads(block):
    both = [block[h * 64 : h * 64 + 64, h * QB : h * QB + QB] for h in range(2)]
    return jnp.concatenate(both, 0).T


def columns(pair, third):
    return slice(third * WIDTH + pair * 128, third * WIDTH + pair * 128 + 128)


def fold(op, parts):
    total = None
    for part in parts:
        for row in range(0, part.shape[0], 8):
            total = part[row : row + 8] if total is None else op(total, part[row : row + 8])
    return total


def pieces_of(size):
    return [slice(0, PAD)] + [slice(PAD + c, PAD + c + CUT) for c in range(0, size, CUT)]


CUT = 32


def attend_step(refs, ends, first, start, count, block):
    mixed, table, attended, totals = refs
    mask = visible(ends, first, start, count)
    rows = pl.ds(pl.multiple_of(first, QB), QB)
    keys = pl.ds(pl.multiple_of(start, QB), count * KC)
    lanes = pl.ds(pl.multiple_of(first, QB), QB)
    cuts = pieces_of(count * KC)

    def score(p):
        return dot_nt(
            jnp.concatenate([table[:, columns(p, 0)], mixed[keys, columns(p, 1)]], 0),
            spread(mixed[rows, columns(p, 0)]),
        )

    def soften(p, scores):
        parts = [scores[cut] + mask[cut] for cut in cuts]
        top = jnp.max(fold(jnp.maximum, parts), 0, keepdims=True)
        low, sums = [], None
        for part in parts:
            raised = jnp.exp(part - top)
            more = fold(jnp.add, [raised])
            sums = more if sums is None else sums + more
            low.append(raised.astype(BF))
        return jnp.concatenate(low, 0), jnp.sum(sums, 0, keepdims=True), top

    def combine(p, low):
        return dot_tn(
            jnp.concatenate([table[:, columns(p, 1)], mixed[keys, columns(p, 2)]], 0), low
        )

    def finish(p, out, total, top):
        log_total = top + jnp.log(total)
        for h in range(2):
            totals[pl.ds(2 * p + h, 1), lanes] = log_total[:, h * QB : h * QB + QB]
        attended[rows, columns(p, 0)] = gather_heads(out * (1.0 / total)).astype(BF)

    scores, soft, outs = {}, {}, {}
    for t in range(PAIRS + AHEAD + 2):
        if t < PAIRS:
            scores[t] = score(t)
        p = t - AHEAD
        if 0 <= p < PAIRS:
            soft[p] = soften(p, scores.pop(p))
            outs[p] = combine(p, soft[p][0])
        p -= 1
        if 0 <= p < PAIRS:
            finish(p, outs.pop(p), *soft.pop(p)[1:])


AHEAD = 3


def attend(mixed, table, lens, row, attended, totals):
    ends = document_ends(lens, row)

    def step(block, carry):
        first, count, start = window(ends, block)
        for size in range(1, STEPS + 1):

            @pl.when(count == size)
            def _():
                attend_step((mixed, table, attended, totals), ends, first, start, size, block)

        return carry

    lax.fori_loop(0, LENGTH // QB, step, 0)


def attend_back_step(refs, ends, first, start, count, block):
    mixed, grad_out, totals, centres, table, grad_mixed, key_sum, value_sum = refs
    mask = visible(ends, first, start, count)
    rows = pl.ds(pl.multiple_of(first, QB), QB)
    keys = pl.ds(pl.multiple_of(start, QB), count * KC)
    lanes = pl.ds(pl.multiple_of(first, QB), QB)
    def row_of(ref, p):
        return jnp.concatenate([ref[pl.ds(2 * p + h, 1), lanes] for h in range(2)], 1)

    cuts = pieces_of(count * KC)
    done = {}

    def products(p):
        query, grad = spread(mixed[rows, columns(p, 0)]), spread(grad_out[rows, columns(p, 0)])
        all_keys = jnp.concatenate([table[:, columns(p, 0)], mixed[keys, columns(p, 1)]], 0)
        all_values = jnp.concatenate([table[:, columns(p, 1)], mixed[keys, columns(p, 2)]], 0)
        return query, grad, all_keys, dot_nt(all_keys, query), dot_nt(all_values, grad)

    def soften(p, scores, grad_probs):
        total, centre = row_of(totals, p), row_of(centres, p)
        low, back = [], []
        for cut in cuts:
            probs = jnp.exp(scores[cut] + (mask[cut] - total))
            low.append(probs.astype(BF))
            back.append((probs * (grad_probs[cut] - centre)).astype(BF))
        return jnp.concatenate(low[1:], 0), jnp.concatenate(back, 0)

    def finish(p, query_grad, key_grad, value_grad):
        grad_mixed[rows, columns(p, 0)] = (gather_heads(query_grad) * 0.125).astype(BF)
        value_sum[keys, columns(p, 0)] += value_grad
        key_sum[keys, columns(p, 0)] += key_grad

    ready, grads = {}, {}
    for t in range(PAIRS + AHEAD_BACK + 2):
        if t < PAIRS:
            ready[t] = products(t)
        p = t - AHEAD_BACK
        if 0 <= p < PAIRS:
            query, grad, all_keys, scores, grad_probs = ready.pop(p)
            low, back = soften(p, scores, grad_probs)
            grads[p] = (dot_tn(all_keys, back), dot(back[PAD:], query), dot(low, grad))
        p -= 1
        if 0 <= p < PAIRS:
            finish(p, *grads.pop(p))


AHEAD_BACK = 2


def attend_back(mixed, grad_out, totals, centres, table, lens, row, grad_mixed, sums, arrive=None):
    ends = document_ends(lens, row)
    key_sum, value_sum = sums

    def clear(index, carry):
        rows = pl.ds(pl.multiple_of(index * 64, 64), 64)
        key_sum[rows, :] = jnp.zeros((64, WIDTH), F32)
        value_sum[rows, :] = jnp.zeros((64, WIDTH), F32)
        return carry

    lax.fori_loop(0, LENGTH // 64, clear, 0)

    def step(block, carry):
        first, count, start = window(ends, block)
        if arrive is not None:
            arrive(block)
        for size in range(1, STEPS + 1):

            @pl.when(count == size)
            def _():
                refs = (mixed, grad_out, totals, centres, table, grad_mixed, key_sum, value_sum)
                attend_back_step(refs, ends, first, start, size, block)

        return carry

    lax.fori_loop(0, LENGTH // QB, step, 0)

    def finish(index, carry):
        rows = pl.ds(pl.multiple_of(index * 64, 64), 64)
        grad_mixed[rows, WIDTH : 2 * WIDTH] = key_sum[rows, :].astype(BF)
        grad_mixed[rows, 2 * WIDTH :] = value_sum[rows, :].astype(BF)
        return carry

    lax.fori_loop(0, LENGTH // 64, finish, 0)


def prefix_back(queries, grad_out, attended, totals, centres, table, grad_table):
    heads = lax.broadcasted_iota(jnp.int32, (HEADS, WIDTH), 0)
    lanes = lax.broadcasted_iota(jnp.int32, (HEADS, WIDTH), 1)
    pick = jnp.where(lanes // 64 == heads, 1.0, 0.0).astype(BF)
    product = attended[...].astype(F32) * grad_out[...].astype(F32)
    centre = dot_nt(pick, product.astype(BF))
    centres[...] = centre
    real = lax.broadcasted_iota(jnp.int32, (4 * PAD, LENGTH), 0) % PAD < PRE
    lane = lax.broadcasted_iota(jnp.int32, (PAD, 256), 1) // 64

    def widen(block):
        zero = jnp.zeros_like(block)
        return jnp.concatenate([jnp.where(lane == h, block, zero) for h in range(4)], 0)

    def narrow(block):
        result = block[:PAD]
        for h in range(1, 4):
            result = jnp.where(lane == h, block[h * PAD : (h + 1) * PAD], result)
        return result

    def repeat(rows):
        return jnp.concatenate(
            [jnp.broadcast_to(rows[h : h + 1], (PAD, LENGTH)) for h in range(4)], 0
        )

    for quad in range(4):
        cols = slice(quad * 256, quad * 256 + 256)
        later = slice(WIDTH + quad * 256, WIDTH + quad * 256 + 256)
        mine = slice(quad * 4, quad * 4 + 4)
        scores = dot_nt(widen(table[:, cols]), queries[:, cols]) - repeat(totals[mine, :])
        probs = jnp.where(real, jnp.exp(scores), 0.0)
        grad_probs = dot_nt(widen(table[:, later]), grad_out[:, cols])
        grad_scores = (probs * (grad_probs - repeat(centre[mine, :]))).astype(BF)
        grad_table[:, cols] = narrow(dot(grad_scores, queries[:, cols]))
        grad_table[:, later] = narrow(dot(probs.astype(BF), grad_out[:, cols]))


def vm(shape, dtype=BF):
    return pltpu.VMEM(shape, dtype)


DMA = pltpu.SemaphoreType.DMA


def wait(copies):
    for copy in copies:
        copy.wait()


def rows_in(source, target, sem, count=4, start=True):
    size = source.shape[0] // count
    copies = [Copy(source.at[tile(r, size)], target.at[tile(r, size)], sem()) for r in range(count)]
    return [copy.start() for copy in copies] if start else copies


def rows_of(source, target, sem, count=4):
    size = source.shape[0] // count
    base = sem.used
    sem.used += count
    return lambda r: Copy(source.at[tile(r, size)], target.at[tile(r, size)], sem.ref.at[base + r])


def picked(pair, target, sem, own, cut=None, count=1):
    if cut is None:
        return [Copy(pair[0], target, sem(), pair[1], own)]
    size = target.shape[cut] // count
    index = [(tile(c, size),) if cut == 0 else (slice(None), tile(c, size)) for c in range(count)]
    return [Copy(pair[0].at[i], target.at[i], sem(), pair[1].at[i], own) for i in index]


def mix_phase(x_v, n_v, w_v, p_v, m_v, waits_x, waits_w, done):
    gain, bias = p_v[GAIN_A : GAIN_A + 1], p_v[BIAS_A : BIAS_A + 1]

    def norm(r):
        wait(waits_x[r] if waits_x else [])
        hat, _ = normalise(x_v[tile(r, 256)].astype(F32))
        n_v[tile(r, 256)] = (hat * gain + bias).astype(BF)

    norm(0)
    for j in range(3):
        wait(waits_w[j])
        cols = tile(j, WIDTH)
        for r in range(4):
            value = dot(n_v[tile(r, 256)], w_v[:, cols]) + p_v[BIAS_M + j : BIAS_M + j + 1]
            value = value.astype(BF)
            if j == 0:
                value = value * jnp.asarray(0.125, BF)
                if r < 3:
                    norm(r + 1)
            m_v[tile(r, 256), cols] = value
    for j in range(3):
        done(j)


def out_phase(x_v, at_v, wo_v, p_v, mid_v, n_v, waits):
    gain, bias = p_v[GAIN_F : GAIN_F + 1], p_v[BIAS_F : BIAS_F + 1]
    for r in range(4):
        rows = tile(r, 256)
        wait(waits[r])
        value = x_v[rows].astype(F32) + dot(at_v[rows], wo_v[...]) + p_v[BIAS_O : BIAS_O + 1]
        mid_v[rows] = value
        hat, _ = normalise(value)
        n_v[rows] = (hat * gain + bias).astype(BF)


def gelu_both(value):
    square = value * value
    half = 0.5 * jnp.tanh(value * (C1 * square + C0)) + 0.5
    result = value * half
    return result, half + result * (1.0 - half) * ((6 * C1) * square + 2 * C0)


def expand_phase(n_v, we_v, p_v, s_v, rows, waits, store):
    for j in range(8):
        cols = tile(j, 512)
        part = tile(j % 2, 512)
        row = BIAS_E + j // 2
        wait(waits.get(j, []))
        value = dot(n_v[rows], we_v[:, cols]) + p_v[row : row + 1, part]
        result, derivative = gelu_both(value)
        store(rows, j, result.astype(BF))
        s_v[rows, cols] = derivative.astype(BF)


def reduce_phase(active, wr_v, p_v, mid_v, o_v, rows, waits):
    wait(waits)
    for n in range(4):
        cols = tile(n, 256)
        value, place = p_v[BIAS_R : BIAS_R + 1, cols], 0
        for ref in active:
            size = ref.shape[1]
            value = value + dot(ref[rows], wr_v[place : place + size, cols])
            place += size
        o_v[rows, cols] = (mid_v[rows, cols] + value).astype(BF)


def feed_back_phase(g_v, s_v, we_v, wr_v, wo_v, p_v, mid_v, go_v, waits, before):
    for r in range(2):
        rows = tile(r, 512)
        total = None
        for c in range(8):
            cols = tile(c, 512)
            if r == 0:
                wait(waits.get(c, []))
            value = dot_nt(g_v[rows], wr_v[cols]) * s_v[rows, cols].astype(F32)
            value = dot_nt(value.astype(BF), we_v[:, cols])
            total = value if total is None else total + value
        if r == 0:
            wait(before)
        gain = p_v[GAIN_F : GAIN_F + 1]
        for half in range(2):
            rows = tile(2 * r + half, 256)
            hat, scale = normalise(mid_v[rows])
            value = norm_back(total[tile(half, 256)], gain, hat, scale)
            value = g_v[rows].astype(F32) + value
            mid_v[rows] = value
            go_v[rows] = dot_nt(value.astype(BF), wo_v[...]).astype(BF)


def mix_back_phase(gm_v, w_v, x_v, mid_v, p_v, o_v, waits, done):
    def step(r):
        rows = tile(r, 256)
        waits(r)
        value = dot_nt(gm_v[rows], w_v[...])
        hat, scale = normalise(x_v[rows].astype(F32))
        value = mid_v[rows] + norm_back(value, p_v[GAIN_A : GAIN_A + 1], hat, scale)
        o_v[rows] = value.astype(BF)
        done(r)

    loop(4, step)


def join_table(pieces, t_v):
    size = pieces.shape[2]
    for index in range(pieces.shape[0]):
        t_v[:, tile(index, size)] = pieces[index].astype(BF)


def cut_table(table, pieces):
    size = pieces.shape[2]
    for index in range(pieces.shape[0]):
        pieces[index] = table[:, tile(index, size)]


def prologue_kernel(
    embed, hidden_weight, hidden_bias, weight, bias, ga, ba, bm, bo, gf, bf, be, br,
    pack, activity, wide, part, e_v,
):
    pack[...] = jnp.zeros(pack.shape, F32)
    row = 0
    for ref in (ga, ba, bm, bo, gf, bf, be, br):
        for index in range(ref.shape[1] // 1024):
            pack[row : row + 1] = ref[:, tile(index, 1024)].astype(F32)
            row += 1
    e_v[...] = jnp.zeros(e_v.shape, F32)
    e_v[:PRE] = embed[...].astype(F32)
    rounded = e_v[...].astype(BF)
    wide[...] = rounded
    act = jnp.tanh(dot(rounded, hidden_weight[...]) + hidden_bias[...].astype(F32)[None])
    activity[...] = act
    value = dot(act.astype(BF), weight[...]) + bias[...].astype(F32)
    part[...] = jnp.broadcast_to(value.astype(BF)[None], part.shape)


def begin(copies):
    return [copy.start() for copy in copies]


def mix_attend_kernel(
    sec, lens, x, table, pack, pack2, w, w2, mixed, attended, totals,
    x_v, n_v, w_v, p_v, m_v, tp_v, t_v, at_v, to_v, sems,
):
    own = sec[0] == 0
    sem = Sems(sems)
    packs = picked((pack, pack2), p_v, sem, own)
    xs = rows_in(x.at[sec[0]], x_v, sem, start=False)
    ws = picked((w, w2), w_v, sem, own, 1, 3)
    tabs = [Copy(table.at[0], tp_v, sem())]
    begin(packs)
    begin(xs[:1])
    begin(ws[:1])
    wait(packs)
    wait(xs[:1])
    begin(xs[1:])
    begin(ws[1:])
    begin(tabs)
    outs = []

    def done(j):
        cols = tile(j, WIDTH)
        outs.append(Copy(m_v.at[:, cols], mixed.at[:, cols], sem()).start())

    mix_phase(x_v, n_v, w_v, p_v, m_v, [[], xs[1:], [], []], [ws[:1], ws[1:], []], done)
    wait(tabs)
    join_table(tp_v, t_v)
    attend(m_v, t_v, lens, sec[0], at_v, to_v)
    outs += [Copy(at_v, attended, sem()).start(), Copy(to_v, totals, sem()).start()]
    wait(outs)


def mix_attend(sec, lens, x, table, packs, weights):
    return call(
        mix_attend_kernel,
        (sec, lens, x, table, *packs, *weights),
        [SMEM, SMEM] + [ANY] * 6,
        [((LENGTH, 3 * WIDTH), BF), ((LENGTH, WIDTH), BF), ((HEADS, LENGTH), F32)],
        [
            vm((LENGTH, WIDTH)), vm((LENGTH, WIDTH)), vm((WIDTH, 3 * WIDTH)), vm((16, 1024), F32),
            vm((LENGTH, 3 * WIDTH)), vm(table.shape[1:], table.dtype), vm((PAD, 2 * WIDTH)),
            vm((LENGTH, WIDTH)), vm((HEADS, LENGTH), F32), DMA((16,)),
        ],
        "mix_attend", 2 * LENGTH * WIDTH * 6 * WIDTH, 20 << 20,
    )


def middle_kernel(
    sec, lens, x, attended, tables, cot, pack, pack2, wm, wm2, wo, wo2, we, we2, wr, wr2,
    keep, send, grad_in, middle, slope, grad_table,
    p0_v, p_v, x_v, n_v, g_v, at_v, wo_v, m_v, mid_v, to_v, tp_v, t_v, c_v, gt_v, sems,
):
    own0, own = sec[0] == 0, sec[0] == 1
    sem = Sems(sems)
    packs = picked((pack, pack2), p0_v, sem, own0) + picked((pack, pack2), p_v, sem, own)
    wos0 = picked((wo, wo2), wo_v, sem, own0)
    wos = picked((wo, wo2), wo_v, sem, own)
    tabs = [Copy(tables.at[1], tp_v, sem())]
    cots = [Copy(cot.at[sec[0]], g_v, sem())]
    grads = rows_of(g_v, grad_in, sem)
    mids = [Copy(mid_v, middle, sem())]
    xs = rows_in(x.at[sec[0]], n_v, sem, start=False)
    ats = rows_in(attended, at_v, sem, start=False)

    def chosen(source, first):
        ends = (keep, send) if first else (send, keep)
        base = sem.used
        sem.used += 4

        def copy(r):
            rows = tile(r, 256)
            choice = [pltpu.make_async_copy(source.at[rows], end.at[rows], sems.at[base + r]) for end in ends]

            class Out:
                def start(self):
                    pl.when(own0)(choice[0].start)
                    pl.when(own)(choice[1].start)

                def wait(self):
                    choice[0].wait()

            return Out()

        return [copy(r) for r in range(4)]

    out0s, out1s = chosen(x_v, True), chosen(n_v, False)

    def mix_scope(wm_v):
        wms = picked((wm, wm2), wm_v, sem, own, 1, 3)

        def first_scope(wr_v, we_v, s_v):
            wes = picked((we, we2), we_v, sem, own0, 1, 8)
            wrs = picked((wr, wr2), wr_v, sem, own0, 1, 4)
            begin(wos0)
            begin(packs)
            begin(ats[:1])
            begin(xs[:1])
            wait(wos0)
            wait(packs)
            begin(ats[1:])
            begin(xs[1:])
            begin(wes)
            waits = [[xs[0], ats[0]], xs[1:] + ats[1:], [], []]
            out_phase(n_v, at_v, wo_v, p0_v, mid_v, n_v, waits)
            begin(mids)
            begin(wos)
            slopes = rows_in(s_v, slope, sem, start=False)

            def store(rows, j, value):
                if j < 6:
                    m_v[rows, tile(j, 512)] = value
                else:
                    at_v[rows, tile(j - 6, 512)] = value

            for r in range(4):
                rows = tile(r, 256)
                expand_phase(n_v, we_v, p0_v, s_v, rows, {0: wes} if r == 0 else {}, store)
                if r == 0:
                    begin(wrs)
            begin(slopes)
            begin(wms)
            begin(tabs)
            for r in range(4):
                rows = tile(r, 256)
                reduce_phase((m_v, at_v), wr_v, p0_v, mid_v, x_v, rows, wrs if r == 0 else [])
            begin(out0s)
            wait(slopes)

        pl.run_scoped(first_scope, vm((FF, WIDTH)), vm((WIDTH, FF)), vm((LENGTH, FF)))
        mix_phase(x_v, n_v, wm_v, p_v, m_v, [], [wms, [], []], lambda j: None)

    pl.run_scoped(mix_scope, vm((WIDTH, 3 * WIDTH)))

    def feed_scope(wr_v, we_v, s_v, a_v):
        wes = picked((we, we2), we_v, sem, own, 1, 8)
        wrs = picked((wr, wr2), wr_v, sem, own, 0, 2)
        wait(tabs)
        begin(wes)
        begin(wrs)
        begin(cots)
        join_table(tp_v, t_v)
        attend(m_v, t_v, lens, sec[0], at_v, to_v)
        wait(wos)
        wait(mids)
        out_phase(x_v, at_v, wo_v, p_v, mid_v, n_v, [[]] * 4)

        def store(rows, j, value):
            a_v[rows, tile(j, 512)] = value

        for r in range(4):
            expand_phase(n_v, we_v, p_v, s_v, tile(r, 256), {0: wes} if r == 0 else {}, store)
        wait(wrs)
        for r in range(4):
            reduce_phase((a_v,), wr_v, p_v, mid_v, n_v, tile(r, 256), [])
        begin(out1s)
        wait(cots)
        feed_back_phase(g_v, s_v, we_v, wr_v, wo_v, p_v, mid_v, n_v, {}, out1s)

    pl.run_scoped(
        feed_scope, vm((FF, WIDTH)), vm((WIDTH, FF)), vm((LENGTH, FF)), vm((LENGTH, FF))
    )
    prefix_back(m_v, n_v, at_v, to_v, c_v, t_v, gt_v)
    table_out = Copy(gt_v, grad_table, sem()).start()

    def attend_scope(gm_v, k_v, v_v, wm_v):
        wms = begin(picked((wm, wm2), wm_v, sem, own))
        attend_back(m_v, n_v, to_v, c_v, t_v, lens, sec[0], gm_v, (k_v, v_v))
        wait(wms)
        mix_back_phase(
            gm_v, wm_v, x_v, mid_v, p_v, g_v, lambda r: None, lambda r: grads(r).start()
        )

    pl.run_scoped(
        attend_scope, vm((LENGTH, 3 * WIDTH)), vm((LENGTH, WIDTH), F32),
        vm((LENGTH, WIDTH), F32), vm((WIDTH, 3 * WIDTH)),
    )

    wait(out0s)
    table_out.wait()
    wait([grads(r) for r in range(4)])


def pack_payload(tables, weight, out):
    pieces, size, part = weight.shape
    each = pieces // 2
    total = jnp.zeros((2 * PAD, size), F32)
    for layer, table in enumerate(tables):
        for index in range(each):
            cols = tile(index, part)
            both = jnp.concatenate(split(table[:, cols]), 0)
            total = total + dot_nt(both, weight[layer * each + index])
            if out.dtype == BF:
                out[layer * each + index, : 2 * PAD] = both
    share = total[:PAD] + total[PAD:]
    if out.dtype == BF:
        rows = [share[:, tile(k, 128)] for k in range(size // 128)]
        shared = jnp.concatenate(rows, 0).astype(BF)
        for index in range(pieces):
            out[index, 2 * PAD :] = shared
    else:
        for layer, table in enumerate(tables):
            out[layer * PAD : (layer + 1) * PAD] = table[...]
        out[2 * PAD :, :size] = share


def middle_part(sec, lens, x, attended, tables, cot, packs, wm, wo, we, wr):
    return call(
        middle_kernel,
        (sec, lens, x, attended, tables, cot, *packs, *wm, *wo, *we, *wr),
        [SMEM, SMEM] + [ANY] * 14,
        [
            ((LENGTH, WIDTH), BF), ((LENGTH, WIDTH), BF), ((LENGTH, WIDTH), BF),
            ((LENGTH, WIDTH), F32), ((LENGTH, FF), BF), ((PAD, 2 * WIDTH), F32),
        ],
        [
            vm((16, 1024), F32), vm((16, 1024), F32), vm((LENGTH, WIDTH)), vm((LENGTH, WIDTH)),
            vm((LENGTH, WIDTH)), vm((LENGTH, WIDTH)), vm((WIDTH, WIDTH)),
            vm((LENGTH, 3 * WIDTH)), vm((LENGTH, WIDTH), F32), vm((HEADS, LENGTH), F32),
            vm(tables.shape[1:], tables.dtype), vm((PAD, 2 * WIDTH)), vm((HEADS, LENGTH), F32),
            vm((PAD, 2 * WIDTH), F32), DMA((80,)),
        ],
        "middle", 2 * LENGTH * WIDTH * 36 * WIDTH, 80 << 20,
    )


def feed_back_kernel(
    sec, g, slope, middle, mixed, attended, totals, table, other, weight, pack, pack2, wo, wo2,
    we, we2, wr, wr2,
    grad_middle, grad_out, centres, payload,
    g_v, s_v, mid_v, q_v, at_v, to_v, tp_v, t_v, p_v, wo_v, we_v, wr_v, go_v, c_v, gt_v, gt0_v,
    pw_v, pay_v, sems,
):
    own = sec[0] == 0
    sem = Sems(sems)
    gs = rows_in(g, g_v, sem, 2, start=False)
    wrs = picked((wr, wr2), wr_v, sem, own, 0, 8)
    wes = picked((we, we2), we_v, sem, own, 1, 8)
    begin(gs[:1])
    parts = []
    for c in range(8):
        cols = tile(c, 512)
        parts.append([wrs[c], Copy(slope.at[:, cols], s_v.at[:, cols], sem()), wes[c]])
    begin(parts[0])
    wait(gs[:1])
    for c in range(1, 8):
        begin(parts[c])
    before = [
        gs[1].start(),
        picked((pack, pack2), p_v, sem, own)[0].start(),
        Copy(middle, mid_v, sem()).start(),
        picked((wo, wo2), wo_v, sem, own)[0].start(),
    ]
    later = [
        Copy(mixed.at[:, :WIDTH], q_v, sem()).start(),
        Copy(attended, at_v, sem()).start(),
        Copy(totals, to_v, sem()).start(),
        Copy(table.at[0], tp_v, sem()).start(),
        Copy(other, gt_v, sem()).start(),
        Copy(weight, pw_v, sem()).start(),
    ]
    groups = {}
    for c, size in ((0, 1), (1, 2), (3, 2), (5, 3)):
        groups[c] = [copy for part in parts[c : c + size] for copy in part]
    feed_back_phase(g_v, s_v, we_v, wr_v, wo_v, p_v, mid_v, go_v, groups, before)
    outs = [Copy(mid_v, grad_middle, sem()).start(), Copy(go_v, grad_out, sem()).start()]
    wait(later)
    join_table(tp_v, t_v)
    prefix_back(q_v, go_v, at_v, to_v, c_v, t_v, gt0_v)
    outs.append(Copy(c_v, centres, sem()).start())
    pack_payload((gt0_v, gt_v), pw_v, pay_v)
    outs.append(Copy(pay_v, payload, sem()).start())
    wait(outs)


def feed_back(sec, g, slope, middle, mixed, attended, totals, table, other, weight, packs, wo, we, wr):
    size = weight.shape[1]
    if weight.shape[2] == 128:
        payload = ((weight.shape[0], 2 * PAD + PAD * size // 128, 128), BF)
    else:
        payload = ((3 * PAD, 2 * WIDTH), F32)
    return call(
        feed_back_kernel,
        (
            sec, g, slope, middle, mixed, attended, totals, table, other, weight, *packs, *wo,
            *we, *wr,
        ),
        [SMEM] + [ANY] * 17,
        [((LENGTH, WIDTH), F32), ((LENGTH, WIDTH), BF), ((HEADS, LENGTH), F32), payload],
        [
            vm((LENGTH, WIDTH)), vm((LENGTH, FF)), vm((LENGTH, WIDTH), F32), vm((LENGTH, WIDTH)),
            vm((LENGTH, WIDTH)), vm((HEADS, LENGTH), F32), vm(table.shape[1:], table.dtype),
            vm((PAD, 2 * WIDTH)), vm((16, 1024), F32),
            vm((WIDTH, WIDTH)), vm((WIDTH, FF)), vm((FF, WIDTH)),
            vm((LENGTH, WIDTH)), vm((HEADS, LENGTH), F32), vm((PAD, 2 * WIDTH), F32),
            vm((PAD, 2 * WIDTH), F32), vm(weight.shape), vm(*payload), DMA((48,)),
        ],
        "feed_back", 2 * LENGTH * WIDTH * 9 * WIDTH, 40 << 20,
    )


def last_kernel(
    sec, lens, mixed, grad_out, totals, centres, table, x, grad_middle, grad1, keep, other,
    pack, pack2, w, w2,
    layer_out, input_grad, send,
    m_v, go_v, to_v, c_v, tp_v, t_v, gm_v, k_v, v_v, b_v, x_v, mid_v, p_v, w_v, o_v, sems,
):
    own = sec[0] == 0
    sem = Sems(sems)
    pairs = ((table.at[0], tp_v), (totals, to_v), (centres, c_v))
    copies = [Copy(a, b, sem()).start() for a, b in pairs]
    blocks = LENGTH // QB
    queries = rows_of(mixed, m_v, sem, blocks)
    outs_in = rows_of(grad_out, go_v, sem, blocks)
    for block in range(blocks):
        queries(block).start()
        outs_in(block).start()
    later = picked((pack, pack2), p_v, sem, own) + picked((w, w2), w_v, sem, own)
    later += [Copy(x.at[sec[0]], x_v, sem()), Copy(grad_middle, mid_v, sem())]
    ins = [
        Copy(keep, b_v.at[0], sem()), Copy(other, b_v.at[1], sem()), Copy(grad1, b_v.at[2], sem())
    ]
    outs = [
        Copy(b_v.at[0], layer_out.at[sec[0]], sem()),
        Copy(b_v.at[1], layer_out.at[1 - sec[0]], sem()),
    ]
    grad1_sem, base = sem(), sem.used
    grad1_outs = [
        pltpu.make_async_copy(b_v.at[2], target, grad1_sem) for target in (send, input_grad.at[1])
    ]
    wait(copies)
    join_table(tp_v, t_v)

    def arrive(block):
        queries(block).wait()
        outs_in(block).wait()

        @pl.when(block == 1)
        def _():
            begin(later)

        @pl.when(block == 3)
        def _():
            begin(ins)

        @pl.when(block == 5)
        def _():
            wait(ins)
            begin(outs)
            pl.when(own)(grad1_outs[0].start)
            pl.when(jnp.logical_not(own))(grad1_outs[1].start)

    attend_back(m_v, go_v, to_v, c_v, t_v, lens, sec[0], gm_v, (k_v, v_v), arrive)
    wait(later)

    def grad0(r):
        rows = tile(r, 256)
        return [
            pltpu.make_async_copy(o_v.at[rows], target.at[rows], sems.at[base + r])
            for target in (input_grad.at[0], send)
        ]

    def done(r):
        pl.when(own)(grad0(r)[0].start)
        pl.when(jnp.logical_not(own))(grad0(r)[1].start)

    mix_back_phase(gm_v, w_v, x_v, mid_v, p_v, o_v, lambda r: None, done)
    wait(outs)
    grad1_outs[0].wait()
    for r in range(4):
        grad0(r)[0].wait()


def last_part(sec, lens, mixed, grad_out, totals, centres, table, x, grad_middle, outs, packs, wm):
    return call(
        last_kernel,
        (sec, lens, mixed, grad_out, totals, centres, table, x, grad_middle, *outs, *packs, *wm),
        [SMEM, SMEM] + [ANY] * 14,
        [((2, LENGTH, WIDTH), BF), ((2, LENGTH, WIDTH), BF), ((LENGTH, WIDTH), BF)],
        [
            vm((LENGTH, 3 * WIDTH)), vm((LENGTH, WIDTH)), vm((HEADS, LENGTH), F32),
            vm((HEADS, LENGTH), F32), vm(table.shape[1:], table.dtype), vm((PAD, 2 * WIDTH)),
            vm((LENGTH, 3 * WIDTH)), vm((LENGTH, WIDTH), F32), vm((LENGTH, WIDTH), F32),
            vm((3, LENGTH, WIDTH)), vm((LENGTH, WIDTH)), vm((LENGTH, WIDTH), F32),
            vm((16, 1024), F32), vm((WIDTH, 3 * WIDTH)), vm((LENGTH, WIDTH)), DMA((48,)),
        ],
        "last", 2 * LENGTH * WIDTH * 13 * WIDTH, 50 << 20,
    )


def place_kernel(sec, other, grads, out, b_v, sems):
    parts = rows_in(other, b_v, Sems(sems.at[pl.ds(0, 4)]), start=False)
    target = out.at[1 - sec[0]]
    outs = rows_in(b_v, target, Sems(sems.at[pl.ds(4, 4)]), start=False)
    begin(parts)
    for r in range(4):
        parts[r].wait()
        outs[r].start()
    wait(outs)


def place(sec, other, grads):
    return pl.pallas_call(
        place_kernel,
        in_specs=[SMEM, ANY, ANY],
        out_specs=ANY,
        out_shape=jax.ShapeDtypeStruct(grads.shape, grads.dtype),
        scratch_shapes=[vm((LENGTH, WIDTH)), DMA((8,))],
        input_output_aliases={2: 0},
        compiler_params=pltpu.CompilerParams(vmem_limit_bytes=62 << 20),
        cost_estimate=pl.CostEstimate(flops=0, bytes_accessed=4 << 20, transcendentals=0),
        name="place",
    )(sec, other, grads)


def prefix_kernel(parts, activity, embed, hidden, ge, gw, gb, gpw, gpb):
    total = parts[0].astype(F32)
    for index in range(1, parts.shape[0]):
        total = total + parts[index].astype(F32)
    act = activity[...]
    share = [total[(2 + k) * PAD : (3 + k) * PAD] for k in range(act.shape[1] // 128)]
    pre = jnp.concatenate(share, 1) * (1.0 - act * act)
    pre = jnp.where(lax.broadcasted_iota(jnp.int32, pre.shape, 0) < PRE, pre, 0.0)
    high, low = split(pre)
    gb[...] = jnp.sum(pre, axis=0, keepdims=True)
    gw[...] = dot_tn(embed[...], high) + dot_tn(embed[...], low)
    ge[...] = dot_nt(high, hidden[...]) + dot_nt(low, hidden[...])
    mine = total[:PAD] + total[PAD : 2 * PAD]
    mine = jnp.where(lax.broadcasted_iota(jnp.int32, mine.shape, 0) < PRE, mine, 0.0)
    high, low = split(mine)
    rounded = act.astype(BF)
    size = gpw.shape[1]
    gpw[...] = (dot_tn(rounded, high) + dot_tn(rounded, low))[:, :size]
    gpb[...] = jnp.sum(mine, axis=0, keepdims=True)[:, :size]


def prefix_grads(parts, activity, embed, hidden, share):
    size = activity.shape[1]
    return call(
        prefix_kernel,
        (parts, activity, embed, hidden),
        [VMEM] * 4,
        [
            ((PAD, WIDTH), F32), ((WIDTH, size), F32), ((1, size), F32), ((size, share), F32),
            ((1, share), F32),
        ],
        [],
        "prefix_grads", 1 << 30, 10 << 20,
        out_specs=[VMEM] * 5,
    )


def per_device(
    inputs, cotangent, doc_lengths, attend_gain, attend_bias, mixing_weight, mixing_bias,
    output_weight, output_bias, feed_gain, feed_bias, expand_weight, expand_bias, reduce_weight,
    reduce_bias, prefix_embed, hidden_weight, hidden_bias, prefix_weight, prefix_bias,
):
    section = lax.axis_index("section")
    sec = section.astype(jnp.int32).reshape(1)
    everyone = ("section", "dp")
    places = lax.axis_size("dp")
    swap = lambda value: lax.ppermute(value, "section", [(0, 1), (1, 0)])
    x = inputs.reshape(2, LENGTH, WIDTH)
    cot = cotangent.reshape(2, LENGTH, WIDTH)
    lens = doc_lengths.reshape(2, DOCS)
    share = prefix_weight.shape[2]

    wm, wo, we, wr = mixing_weight[0], output_weight[0], expand_weight[0], reduce_weight[0]
    wm2 = swap(wm)
    vectors = (
        attend_gain, attend_bias, mixing_bias, output_bias, feed_gain, feed_bias, expand_bias,
        reduce_bias,
    )
    pack, activity, embed, part = call(
        prologue_kernel,
        (prefix_embed, hidden_weight, hidden_bias, prefix_weight[0], prefix_bias, *vectors),
        [VMEM] * 13,
        [
            ((16, 1024), F32), ((PAD, hidden_weight.shape[1]), F32), ((PAD, WIDTH), BF),
            ((2 * places, PAD, share), BF),
        ],
        [vm((PAD, WIDTH), F32)],
        "prologue", 1 << 24, 2 << 20,
        out_specs=[VMEM] * 4,
    )
    pack2 = swap(pack)

    tables = lax.all_to_all(part, everyone, 0, 0)
    tables = tables.reshape(2, places, PAD, share)
    if share % 128:
        tables = tables.transpose(0, 2, 1, 3).reshape(2, 1, PAD, 2 * WIDTH)
    full = lax.all_gather(prefix_weight[0], everyone, axis=0)
    if share != 128:
        full = full.reshape(2, places, -1, share).transpose(0, 2, 1, 3)
        full = full.reshape(2, -1, 2 * WIDTH)
    wo_in, we_in, wr_in, wm2 = lax.optimization_barrier((wo, we, wr, wm2))
    wo2, we2, wr2 = swap(wo_in), swap(we_in), swap(wr_in)
    wm2, pack2, tables = lax.optimization_barrier((wm2, pack2, tables))
    packs = (pack, pack2)
    wms, wos, wes, wrs = (wm, wm2), (wo, wo2), (we, we2), (wr, wr2)

    mixed, attended, totals = mix_attend(sec, lens, x, tables, packs, wms)
    keep, send, grad1, middle, slope, table_grad1 = middle_part(
        sec, lens, x, attended, tables, cot, packs, wms, wos, wes, wrs
    )
    other = swap(send)
    grad_middle, grad_out, centres, payload = feed_back(
        sec, grad1, slope, middle, mixed, attended, totals, tables, table_grad1, full, packs,
        wos, wes, wrs,
    )

    if share != 128:
        table_grads = jnp.stack(split(payload[: 2 * PAD].reshape(2, PAD, places, share)), 0)
        table_grads = table_grads.transpose(1, 3, 0, 2, 4).reshape(2 * places, 2 * PAD, share)
        table_grads = jnp.pad(table_grads, ((0, 0), (0, 0), (0, 128 - share)))
        units = payload[2 * PAD :, : activity.shape[1]].reshape(PAD, -1, 128).transpose(1, 0, 2)
        units = jnp.broadcast_to(units.astype(BF).reshape(1, -1, 128), (2 * places, units.size // 128, 128))
        payload = jnp.concatenate([table_grads, units], 1)
    parts = lax.all_to_all(payload, everyone, 0, 0)
    layer_out, grads, send = last_part(
        sec, lens, mixed, grad_out, totals, centres, tables, x, grad_middle,
        (grad1, keep, other), packs, wms,
    )
    parts, send, grads = lax.optimization_barrier((parts, send, grads))
    other = swap(send)
    ge, gw, gb, gpw, gpb = prefix_grads(parts, activity, embed, hidden_weight, share)
    input_grad = place(sec, other, grads)
    shape = (1, 2, 1, LENGTH, WIDTH)
    return (
        layer_out.reshape(shape), input_grad.reshape(shape), ge[:PRE], gw, gb[0], gpw[None], gpb
    )


def solution(mesh):
    in_specs = (
        P(None, "dp", None, None),
        P(None, "dp", None, None),
        P(None, "dp", None),
        P("section", None),
        P("section", None),
        P("section", None, None),
        P("section", None),
        P("section", None, None),
        P("section", None),
        P("section", None),
        P("section", None),
        P("section", None, None),
        P("section", None),
        P("section", None, None),
        P("section", None),
        P(),
        P(),
        P(),
        P("section", None, "dp"),
        P("section", "dp"),
    )
    out_specs = (
        P("section", None, "dp", None, None),
        P("section", None, "dp", None, None),
        P(),
        P(),
        P(),
        P("section", None, "dp"),
        P("section", "dp"),
    )
    return jax.shard_map(
        per_device, mesh=mesh, in_specs=in_specs, out_specs=out_specs, check_vma=False
    )
```

```python
import jax
import jax.numpy as jnp
from jax import lax
from jax.experimental import pallas as pl
from jax.experimental.pallas import tpu as pltpu
from jax.sharding import PartitionSpec as P

F32 = jnp.float32
BF = jnp.bfloat16
LENGTH = 1024
WIDTH = 1024
FF = 4096
HEADS = 16
PRE = 10
PAD = 16
DOCS = 8
QB = 128
KC = 128
PAIRS = 8
STEPS = 5
NEG = -1e9
C0 = 0.7978845608028654
C1 = C0 * 0.044715

ANY = pl.BlockSpec(memory_space=pl.ANY)
SMEM = pl.BlockSpec(memory_space=pltpu.SMEM)
VMEM = pl.BlockSpec(memory_space=pltpu.VMEM)


def dot(a, b):
    return jnp.dot(a, b, preferred_element_type=F32)


def dot_nt(a, b):
    return lax.dot_general(a, b, (((1,), (1,)), ((), ())), preferred_element_type=F32)


def dot_tn(a, b):
    return lax.dot_general(a, b, (((0,), (0,)), ((), ())), preferred_element_type=F32)


def split(value):
    high = value.astype(BF)
    return high, (value - high.astype(F32)).astype(BF)


def call(kernel, ins, in_specs, outs, scratch, name, flops=0, moved=0, out_specs=None):
    return pl.pallas_call(
        kernel,
        in_specs=in_specs,
        out_specs=out_specs or [ANY] * len(outs),
        out_shape=[jax.ShapeDtypeStruct(s, d) for s, d in outs],
        scratch_shapes=scratch,
        compiler_params=pltpu.CompilerParams(vmem_limit_bytes=62 << 20),
        cost_estimate=pl.CostEstimate(flops=flops, bytes_accessed=moved, transcendentals=0),
        name=name,
    )(*ins)


class Copy:
    def __init__(self, source, target, sem, other=None, own=None):
        self.first = pltpu.make_async_copy(source, target, sem)
        self.second = None if other is None else pltpu.make_async_copy(other, target, sem)
        self.own = own

    def start(self):
        if self.second is None:
            self.first.start()
        else:
            pl.when(self.own)(self.first.start)
            pl.when(jnp.logical_not(self.own))(self.second.start)
        return self

    def wait(self):
        self.first.wait()


class Sems:
    def __init__(self, ref):
        self.ref = ref
        self.used = 0

    def __call__(self):
        self.used += 1
        return self.ref.at[self.used - 1]


GAIN_A, BIAS_A, BIAS_M, BIAS_O, GAIN_F, BIAS_F, BIAS_E, BIAS_R = 0, 1, 2, 5, 6, 7, 8, 12


def tile(index, rows):
    if isinstance(index, int):
        return slice(index * rows, (index + 1) * rows)
    return pl.ds(pl.multiple_of(index * rows, rows), rows)


def loop(count, body):
    def step(index, carry):
        body(index)
        return carry

    lax.fori_loop(0, count, step, 0)


def normalise(values):
    centre = jnp.mean(values, axis=-1, keepdims=True)
    shifted = values - centre
    variance = jnp.mean(shifted * shifted, axis=-1, keepdims=True)
    scale = lax.rsqrt(variance + 1e-5)
    return shifted * scale, scale


def norm_back(grad, gain, hat, scale):
    weighted = grad * gain
    first = jnp.mean(weighted, axis=-1, keepdims=True)
    second = jnp.mean(weighted * hat, axis=-1, keepdims=True)
    return scale * (weighted - first - hat * second)


def document_ends(lens, row):
    ends, total = [], None
    for doc in range(DOCS - 1):
        total = lens[row, doc] if total is None else total + lens[row, doc]
        ends.append(total)
    return ends


def window(ends, block):
    first = block * QB
    low = jnp.int32(0)
    for end in ends:
        low = jnp.maximum(low, jnp.where(first >= end, end, 0))
    count = (first + QB - low + KC - 1) // KC
    start = jnp.maximum(first + QB - count * KC, 0)
    return first, count, start


def visible(ends, first, start, count):
    places = first + lax.broadcasted_iota(jnp.int32, (1, QB), 1)
    low = jnp.zeros((1, QB), jnp.int32)
    for end in ends:
        low = jnp.maximum(low, jnp.where(places >= end, end, 0))
    keys = start + lax.broadcasted_iota(jnp.int32, (count * KC, QB), 0)
    inside = jnp.where((keys <= places) & (keys >= low), 0.0, NEG).astype(F32)
    prefix = lax.broadcasted_iota(jnp.int32, (PAD, QB), 0)
    prefix = jnp.where(prefix < PRE, 0.0, NEG).astype(F32)
    mask = jnp.concatenate([prefix, inside], 0)
    return jnp.concatenate([mask, mask], 1)


def spread(block):
    lane = lax.broadcasted_iota(jnp.int32, block.shape, 1) // 64
    zero = jnp.zeros_like(block)
    return jnp.concatenate([jnp.where(lane == h, block, zero) for h in range(2)], 0)


def gather_heads(block):
    both = [block[h * 64 : h * 64 + 64, h * QB : h * QB + QB] for h in range(2)]
    return jnp.concatenate(both, 0).T


def columns(pair, third):
    return slice(third * WIDTH + pair * 128, third * WIDTH + pair * 128 + 128)


def fold(op, parts):
    total = None
    for part in parts:
        for row in range(0, part.shape[0], 8):
            total = part[row : row + 8] if total is None else op(total, part[row : row + 8])
    return total


def pieces_of(size):
    return [slice(0, PAD)] + [slice(PAD + c, PAD + c + CUT) for c in range(0, size, CUT)]


CUT = 32


def attend_step(refs, ends, first, start, count, block):
    mixed, table, attended, totals = refs
    mask = visible(ends, first, start, count)
    rows = pl.ds(pl.multiple_of(first, QB), QB)
    keys = pl.ds(pl.multiple_of(start, QB), count * KC)
    lanes = pl.ds(pl.multiple_of(first, QB), QB)
    cuts = pieces_of(count * KC)

    def score(p):
        return dot_nt(
            jnp.concatenate([table[:, columns(p, 0)], mixed[keys, columns(p, 1)]], 0),
            spread(mixed[rows, columns(p, 0)]),
        )

    def soften(p, scores):
        parts = [scores[cut] + mask[cut] for cut in cuts]
        top = jnp.max(fold(jnp.maximum, parts), 0, keepdims=True)
        low, sums = [], None
        for part in parts:
            raised = jnp.exp(part - top)
            more = fold(jnp.add, [raised])
            sums = more if sums is None else sums + more
            low.append(raised.astype(BF))
        return jnp.concatenate(low, 0), jnp.sum(sums, 0, keepdims=True), top

    def combine(p, low):
        return dot_tn(
            jnp.concatenate([table[:, columns(p, 1)], mixed[keys, columns(p, 2)]], 0), low
        )

    def finish(p, out, total, top):
        log_total = top + jnp.log(total)
        for h in range(2):
            totals[pl.ds(2 * p + h, 1), lanes] = log_total[:, h * QB : h * QB + QB]
        attended[rows, columns(p, 0)] = gather_heads(out * (1.0 / total)).astype(BF)

    scores, soft, outs = {}, {}, {}
    for t in range(PAIRS + AHEAD + 2):
        if t < PAIRS:
            scores[t] = score(t)
        p = t - AHEAD
        if 0 <= p < PAIRS:
            soft[p] = soften(p, scores.pop(p))
            outs[p] = combine(p, soft[p][0])
        p -= 1
        if 0 <= p < PAIRS:
            finish(p, outs.pop(p), *soft.pop(p)[1:])


AHEAD = 3


def attend(mixed, table, lens, row, attended, totals):
    ends = document_ends(lens, row)

    def step(block, carry):
        first, count, start = window(ends, block)
        for size in range(1, STEPS + 1):

            @pl.when(count == size)
            def _():
                attend_step((mixed, table, attended, totals), ends, first, start, size, block)

        return carry

    lax.fori_loop(0, LENGTH // QB, step, 0)


def attend_back_step(refs, ends, first, start, count, block):
    mixed, grad_out, totals, centres, table, grad_mixed, key_sum, value_sum = refs
    mask = visible(ends, first, start, count)
    rows = pl.ds(pl.multiple_of(first, QB), QB)
    keys = pl.ds(pl.multiple_of(start, QB), count * KC)
    lanes = pl.ds(pl.multiple_of(first, QB), QB)
    def row_of(ref, p):
        return jnp.concatenate([ref[pl.ds(2 * p + h, 1), lanes] for h in range(2)], 1)

    cuts = pieces_of(count * KC)
    done = {}

    def products(p):
        query, grad = spread(mixed[rows, columns(p, 0)]), spread(grad_out[rows, columns(p, 0)])
        all_keys = jnp.concatenate([table[:, columns(p, 0)], mixed[keys, columns(p, 1)]], 0)
        all_values = jnp.concatenate([table[:, columns(p, 1)], mixed[keys, columns(p, 2)]], 0)
        return query, grad, all_keys, dot_nt(all_keys, query), dot_nt(all_values, grad)

    def soften(p, scores, grad_probs):
        total, centre = row_of(totals, p), row_of(centres, p)
        low, back = [], []
        for cut in cuts:
            probs = jnp.exp(scores[cut] + (mask[cut] - total))
            low.append(probs.astype(BF))
            back.append((probs * (grad_probs[cut] - centre)).astype(BF))
        return jnp.concatenate(low[1:], 0), jnp.concatenate(back, 0)

    def finish(p, query_grad, key_grad, value_grad):
        grad_mixed[rows, columns(p, 0)] = (gather_heads(query_grad) * 0.125).astype(BF)
        value_sum[keys, columns(p, 0)] += value_grad
        key_sum[keys, columns(p, 0)] += key_grad

    ready, grads = {}, {}
    for t in range(PAIRS + AHEAD_BACK + 2):
        if t < PAIRS:
            ready[t] = products(t)
        p = t - AHEAD_BACK
        if 0 <= p < PAIRS:
            query, grad, all_keys, scores, grad_probs = ready.pop(p)
            low, back = soften(p, scores, grad_probs)
            grads[p] = (dot_tn(all_keys, back), dot(back[PAD:], query), dot(low, grad))
        p -= 1
        if 0 <= p < PAIRS:
            finish(p, *grads.pop(p))


AHEAD_BACK = 2


def attend_back(mixed, grad_out, totals, centres, table, lens, row, grad_mixed, sums, arrive=None):
    ends = document_ends(lens, row)
    key_sum, value_sum = sums

    def clear(index, carry):
        rows = pl.ds(pl.multiple_of(index * 64, 64), 64)
        key_sum[rows, :] = jnp.zeros((64, WIDTH), F32)
        value_sum[rows, :] = jnp.zeros((64, WIDTH), F32)
        return carry

    lax.fori_loop(0, LENGTH // 64, clear, 0)

    def step(block, carry):
        first, count, start = window(ends, block)
        if arrive is not None:
            arrive(block)
        for size in range(1, STEPS + 1):

            @pl.when(count == size)
            def _():
                refs = (mixed, grad_out, totals, centres, table, grad_mixed, key_sum, value_sum)
                attend_back_step(refs, ends, first, start, size, block)

        return carry

    lax.fori_loop(0, LENGTH // QB, step, 0)

    def finish(index, carry):
        rows = pl.ds(pl.multiple_of(index * 64, 64), 64)
        grad_mixed[rows, WIDTH : 2 * WIDTH] = key_sum[rows, :].astype(BF)
        grad_mixed[rows, 2 * WIDTH :] = value_sum[rows, :].astype(BF)
        return carry

    lax.fori_loop(0, LENGTH // 64, finish, 0)


def prefix_back(queries, grad_out, attended, totals, centres, table, grad_table):
    heads = lax.broadcasted_iota(jnp.int32, (HEADS, WIDTH), 0)
    lanes = lax.broadcasted_iota(jnp.int32, (HEADS, WIDTH), 1)
    pick = jnp.where(lanes // 64 == heads, 1.0, 0.0).astype(BF)
    product = attended[...].astype(F32) * grad_out[...].astype(F32)
    centre = dot_nt(pick, product.astype(BF))
    centres[...] = centre
    real = lax.broadcasted_iota(jnp.int32, (4 * PAD, LENGTH), 0) % PAD < PRE
    lane = lax.broadcasted_iota(jnp.int32, (PAD, 256), 1) // 64

    def widen(block):
        zero = jnp.zeros_like(block)
        return jnp.concatenate([jnp.where(lane == h, block, zero) for h in range(4)], 0)

    def narrow(block):
        result = block[:PAD]
        for h in range(1, 4):
            result = jnp.where(lane == h, block[h * PAD : (h + 1) * PAD], result)
        return result

    def repeat(rows):
        return jnp.concatenate(
            [jnp.broadcast_to(rows[h : h + 1], (PAD, LENGTH)) for h in range(4)], 0
        )

    for quad in range(4):
        cols = slice(quad * 256, quad * 256 + 256)
        later = slice(WIDTH + quad * 256, WIDTH + quad * 256 + 256)
        mine = slice(quad * 4, quad * 4 + 4)
        scores = dot_nt(widen(table[:, cols]), queries[:, cols]) - repeat(totals[mine, :])
        probs = jnp.where(real, jnp.exp(scores), 0.0)
        grad_probs = dot_nt(widen(table[:, later]), grad_out[:, cols])
        grad_scores = (probs * (grad_probs - repeat(centre[mine, :]))).astype(BF)
        grad_table[:, cols] = narrow(dot(grad_scores, queries[:, cols]))
        grad_table[:, later] = narrow(dot(probs.astype(BF), grad_out[:, cols]))


def vm(shape, dtype=BF):
    return pltpu.VMEM(shape, dtype)


DMA = pltpu.SemaphoreType.DMA


def wait(copies):
    for copy in copies:
        copy.wait()


def rows_in(source, target, sem, count=4, start=True):
    size = source.shape[0] // count
    copies = [Copy(source.at[tile(r, size)], target.at[tile(r, size)], sem()) for r in range(count)]
    return [copy.start() for copy in copies] if start else copies


def rows_of(source, target, sem, count=4):
    size = source.shape[0] // count
    base = sem.used
    sem.used += count
    return lambda r: Copy(source.at[tile(r, size)], target.at[tile(r, size)], sem.ref.at[base + r])


def picked(pair, target, sem, own, cut=None, count=1):
    if cut is None:
        return [Copy(pair[0], target, sem(), pair[1], own)]
    size = target.shape[cut] // count
    index = [(tile(c, size),) if cut == 0 else (slice(None), tile(c, size)) for c in range(count)]
    return [Copy(pair[0].at[i], target.at[i], sem(), pair[1].at[i], own) for i in index]


def mix_phase(x_v, n_v, w_v, p_v, m_v, waits_x, waits_w, done):
    gain, bias = p_v[GAIN_A : GAIN_A + 1], p_v[BIAS_A : BIAS_A + 1]

    def norm(r):
        wait(waits_x[r] if waits_x else [])
        hat, _ = normalise(x_v[tile(r, 256)].astype(F32))
        n_v[tile(r, 256)] = (hat * gain + bias).astype(BF)

    norm(0)
    for j in range(3):
        wait(waits_w[j])
        cols = tile(j, WIDTH)
        for r in range(4):
            value = dot(n_v[tile(r, 256)], w_v[:, cols]) + p_v[BIAS_M + j : BIAS_M + j + 1]
            value = value.astype(BF)
            if j == 0:
                value = value * jnp.asarray(0.125, BF)
                if r < 3:
                    norm(r + 1)
            m_v[tile(r, 256), cols] = value
    for j in range(3):
        done(j)


def out_phase(x_v, at_v, wo_v, p_v, mid_v, n_v, waits):
    gain, bias = p_v[GAIN_F : GAIN_F + 1], p_v[BIAS_F : BIAS_F + 1]
    for r in range(4):
        rows = tile(r, 256)
        wait(waits[r])
        value = x_v[rows].astype(F32) + dot(at_v[rows], wo_v[...]) + p_v[BIAS_O : BIAS_O + 1]
        mid_v[rows] = value
        hat, _ = normalise(value)
        n_v[rows] = (hat * gain + bias).astype(BF)


def gelu_both(value):
    square = value * value
    half = 0.5 * jnp.tanh(value * (C1 * square + C0)) + 0.5
    result = value * half
    return result, half + result * (1.0 - half) * ((6 * C1) * square + 2 * C0)


def expand_phase(n_v, we_v, p_v, s_v, rows, waits, store):
    for j in range(8):
        cols = tile(j, 512)
        part = tile(j % 2, 512)
        row = BIAS_E + j // 2
        wait(waits.get(j, []))
        value = dot(n_v[rows], we_v[:, cols]) + p_v[row : row + 1, part]
        result, derivative = gelu_both(value)
        store(rows, j, result.astype(BF))
        s_v[rows, cols] = derivative.astype(BF)


def reduce_phase(active, wr_v, p_v, mid_v, o_v, rows, waits):
    wait(waits)
    for n in range(4):
        cols = tile(n, 256)
        value, place = p_v[BIAS_R : BIAS_R + 1, cols], 0
        for ref in active:
            size = ref.shape[1]
            value = value + dot(ref[rows], wr_v[place : place + size, cols])
            place += size
        o_v[rows, cols] = (mid_v[rows, cols] + value).astype(BF)


def feed_back_phase(g_v, s_v, we_v, wr_v, wo_v, p_v, mid_v, go_v, waits, before):
    for r in range(2):
        rows = tile(r, 512)
        total = None
        for c in range(8):
            cols = tile(c, 512)
            if r == 0:
                wait(waits.get(c, []))
            value = dot_nt(g_v[rows], wr_v[cols]) * s_v[rows, cols].astype(F32)
            value = dot_nt(value.astype(BF), we_v[:, cols])
            total = value if total is None else total + value
        if r == 0:
            wait(before)
        gain = p_v[GAIN_F : GAIN_F + 1]
        for half in range(2):
            rows = tile(2 * r + half, 256)
            hat, scale = normalise(mid_v[rows])
            value = norm_back(total[tile(half, 256)], gain, hat, scale)
            value = g_v[rows].astype(F32) + value
            mid_v[rows] = value
            go_v[rows] = dot_nt(value.astype(BF), wo_v[...]).astype(BF)


def mix_back_phase(gm_v, w_v, x_v, mid_v, p_v, o_v, waits, done):
    def step(r):
        rows = tile(r, 256)
        waits(r)
        value = dot_nt(gm_v[rows], w_v[...])
        hat, scale = normalise(x_v[rows].astype(F32))
        value = mid_v[rows] + norm_back(value, p_v[GAIN_A : GAIN_A + 1], hat, scale)
        o_v[rows] = value.astype(BF)
        done(r)

    loop(4, step)


def join_table(pieces, t_v):
    size = pieces.shape[2]
    for index in range(pieces.shape[0]):
        t_v[:, tile(index, size)] = pieces[index].astype(BF)


def cut_table(table, pieces):
    size = pieces.shape[2]
    for index in range(pieces.shape[0]):
        pieces[index] = table[:, tile(index, size)]


def prologue_kernel(
    embed, hidden_weight, hidden_bias, weight, bias, ga, ba, bm, bo, gf, bf, be, br,
    pack, activity, wide, part, e_v,
):
    pack[...] = jnp.zeros(pack.shape, F32)
    row = 0
    for ref in (ga, ba, bm, bo, gf, bf, be, br):
        for index in range(ref.shape[1] // 1024):
            pack[row : row + 1] = ref[:, tile(index, 1024)].astype(F32)
            row += 1
    e_v[...] = jnp.zeros(e_v.shape, F32)
    e_v[:PRE] = embed[...].astype(F32)
    rounded = e_v[...].astype(BF)
    wide[...] = rounded
    act = jnp.tanh(dot(rounded, hidden_weight[...]) + hidden_bias[...].astype(F32)[None])
    activity[...] = act
    value = dot(act.astype(BF), weight[...]) + bias[...].astype(F32)
    part[...] = jnp.broadcast_to(value.astype(BF)[None], part.shape)


def begin(copies):
    return [copy.start() for copy in copies]


def mix_attend_kernel(
    sec, lens, x, table, pack, pack2, w, w2, mixed, attended, totals,
    x_v, n_v, w_v, p_v, m_v, tp_v, t_v, at_v, to_v, sems,
):
    own = sec[0] == 0
    sem = Sems(sems)
    packs = picked((pack, pack2), p_v, sem, own)
    xs = rows_in(x.at[sec[0]], x_v, sem, start=False)
    ws = picked((w, w2), w_v, sem, own, 1, 3)
    tabs = [Copy(table.at[0], tp_v, sem())]
    begin(packs)
    begin(xs[:1])
    begin(ws[:1])
    wait(packs)
    wait(xs[:1])
    begin(xs[1:])
    begin(ws[1:])
    begin(tabs)
    outs = []

    def done(j):
        cols = tile(j, WIDTH)
        outs.append(Copy(m_v.at[:, cols], mixed.at[:, cols], sem()).start())

    mix_phase(x_v, n_v, w_v, p_v, m_v, [[], xs[1:], [], []], [ws[:1], ws[1:], []], done)
    wait(tabs)
    join_table(tp_v, t_v)
    attend(m_v, t_v, lens, sec[0], at_v, to_v)
    outs += [Copy(at_v, attended, sem()).start(), Copy(to_v, totals, sem()).start()]
    wait(outs)


def mix_attend(sec, lens, x, table, packs, weights):
    return call(
        mix_attend_kernel,
        (sec, lens, x, table, *packs, *weights),
        [SMEM, SMEM] + [ANY] * 6,
        [((LENGTH, 3 * WIDTH), BF), ((LENGTH, WIDTH), BF), ((HEADS, LENGTH), F32)],
        [
            vm((LENGTH, WIDTH)), vm((LENGTH, WIDTH)), vm((WIDTH, 3 * WIDTH)), vm((16, 1024), F32),
            vm((LENGTH, 3 * WIDTH)), vm(table.shape[1:], table.dtype), vm((PAD, 2 * WIDTH)),
            vm((LENGTH, WIDTH)), vm((HEADS, LENGTH), F32), DMA((16,)),
        ],
        "mix_attend", 2 * LENGTH * WIDTH * 6 * WIDTH, 20 << 20,
    )


def middle_kernel(
    sec, lens, x, attended, tables, cot, pack, pack2, wm, wm2, wo, wo2, we, we2, wr, wr2,
    keep, send, grad_in, middle, slope, grad_table,
    p0_v, p_v, x_v, n_v, g_v, at_v, wo_v, m_v, mid_v, to_v, tp_v, t_v, c_v, gt_v, sems,
):
    own0, own = sec[0] == 0, sec[0] == 1
    sem = Sems(sems)
    packs = picked((pack, pack2), p0_v, sem, own0) + picked((pack, pack2), p_v, sem, own)
    wos0 = picked((wo, wo2), wo_v, sem, own0)
    wos = picked((wo, wo2), wo_v, sem, own)
    tabs = [Copy(tables.at[1], tp_v, sem())]
    cots = [Copy(cot.at[sec[0]], g_v, sem())]
    grads = rows_of(g_v, grad_in, sem)
    mids = [Copy(mid_v, middle, sem())]
    xs = rows_in(x.at[sec[0]], n_v, sem, start=False)
    ats = rows_in(attended, at_v, sem, start=False)

    def chosen(source, first):
        ends = (keep, send) if first else (send, keep)
        base = sem.used
        sem.used += 4

        def copy(r):
            rows = tile(r, 256)
            choice = [pltpu.make_async_copy(source.at[rows], end.at[rows], sems.at[base + r]) for end in ends]

            class Out:
                def start(self):
                    pl.when(own0)(choice[0].start)
                    pl.when(own)(choice[1].start)

                def wait(self):
                    choice[0].wait()

            return Out()

        return [copy(r) for r in range(4)]

    out0s, out1s = chosen(x_v, True), chosen(n_v, False)

    def mix_scope(wm_v):
        wms = picked((wm, wm2), wm_v, sem, own, 1, 3)

        def first_scope(wr_v, we_v, s_v):
            wes = picked((we, we2), we_v, sem, own0, 1, 8)
            wrs = picked((wr, wr2), wr_v, sem, own0, 1, 4)
            begin(wos0)
            begin(packs)
            begin(ats[:1])
            begin(xs[:1])
            wait(wos0)
            wait(packs)
            begin(ats[1:])
            begin(xs[1:])
            begin(wes)
            waits = [[xs[0], ats[0]], xs[1:] + ats[1:], [], []]
            out_phase(n_v, at_v, wo_v, p0_v, mid_v, n_v, waits)
            begin(mids)
            begin(wos)
            slopes = rows_in(s_v, slope, sem, start=False)

            def store(rows, j, value):
                if j < 6:
                    m_v[rows, tile(j, 512)] = value
                else:
                    at_v[rows, tile(j - 6, 512)] = value

            for r in range(4):
                rows = tile(r, 256)
                expand_phase(n_v, we_v, p0_v, s_v, rows, {0: wes} if r == 0 else {}, store)
                if r == 0:
                    begin(wrs)
            begin(slopes)
            begin(wms)
            begin(tabs)
            for r in range(4):
                rows = tile(r, 256)
                reduce_phase((m_v, at_v), wr_v, p0_v, mid_v, x_v, rows, wrs if r == 0 else [])
            begin(out0s)
            wait(slopes)

        pl.run_scoped(first_scope, vm((FF, WIDTH)), vm((WIDTH, FF)), vm((LENGTH, FF)))
        mix_phase(x_v, n_v, wm_v, p_v, m_v, [], [wms, [], []], lambda j: None)

    pl.run_scoped(mix_scope, vm((WIDTH, 3 * WIDTH)))

    def feed_scope(wr_v, we_v, s_v, a_v):
        wes = picked((we, we2), we_v, sem, own, 1, 8)
        wrs = picked((wr, wr2), wr_v, sem, own, 0, 2)
        wait(tabs)
        begin(wes)
        begin(wrs)
        begin(cots)
        join_table(tp_v, t_v)
        attend(m_v, t_v, lens, sec[0], at_v, to_v)
        wait(wos)
        wait(mids)
        out_phase(x_v, at_v, wo_v, p_v, mid_v, n_v, [[]] * 4)

        def store(rows, j, value):
            a_v[rows, tile(j, 512)] = value

        for r in range(4):
            expand_phase(n_v, we_v, p_v, s_v, tile(r, 256), {0: wes} if r == 0 else {}, store)
        wait(wrs)
        for r in range(4):
            reduce_phase((a_v,), wr_v, p_v, mid_v, n_v, tile(r, 256), [])
        begin(out1s)
        wait(cots)
        feed_back_phase(g_v, s_v, we_v, wr_v, wo_v, p_v, mid_v, n_v, {}, out1s)

    pl.run_scoped(
        feed_scope, vm((FF, WIDTH)), vm((WIDTH, FF)), vm((LENGTH, FF)), vm((LENGTH, FF))
    )
    prefix_back(m_v, n_v, at_v, to_v, c_v, t_v, gt_v)
    table_out = Copy(gt_v, grad_table, sem()).start()

    def attend_scope(gm_v, k_v, v_v, wm_v):
        wms = begin(picked((wm, wm2), wm_v, sem, own))
        attend_back(m_v, n_v, to_v, c_v, t_v, lens, sec[0], gm_v, (k_v, v_v))
        wait(wms)
        mix_back_phase(
            gm_v, wm_v, x_v, mid_v, p_v, g_v, lambda r: None, lambda r: grads(r).start()
        )

    pl.run_scoped(
        attend_scope, vm((LENGTH, 3 * WIDTH)), vm((LENGTH, WIDTH), F32),
        vm((LENGTH, WIDTH), F32), vm((WIDTH, 3 * WIDTH)),
    )

    wait(out0s)
    table_out.wait()
    wait([grads(r) for r in range(4)])


def pack_payload(tables, weight, out):
    pieces, size, part = weight.shape
    each = pieces // 2
    total = jnp.zeros((2 * PAD, size), F32)
    for layer, table in enumerate(tables):
        for index in range(each):
            cols = tile(index, part)
            both = jnp.concatenate(split(table[:, cols]), 0)
            total = total + dot_nt(both, weight[layer * each + index])
            if out.dtype == BF:
                out[layer * each + index, : 2 * PAD] = both
    share = total[:PAD] + total[PAD:]
    if out.dtype == BF:
        rows = [share[:, tile(k, 128)] for k in range(size // 128)]
        shared = jnp.concatenate(rows, 0).astype(BF)
        for index in range(pieces):
            out[index, 2 * PAD :] = shared
    else:
        for layer, table in enumerate(tables):
            out[layer * PAD : (layer + 1) * PAD] = table[...]
        out[2 * PAD :, :size] = share


def middle_part(sec, lens, x, attended, tables, cot, packs, wm, wo, we, wr):
    return call(
        middle_kernel,
        (sec, lens, x, attended, tables, cot, *packs, *wm, *wo, *we, *wr),
        [SMEM, SMEM] + [ANY] * 14,
        [
            ((LENGTH, WIDTH), BF), ((LENGTH, WIDTH), BF), ((LENGTH, WIDTH), BF),
            ((LENGTH, WIDTH), F32), ((LENGTH, FF), BF), ((PAD, 2 * WIDTH), F32),
        ],
        [
            vm((16, 1024), F32), vm((16, 1024), F32), vm((LENGTH, WIDTH)), vm((LENGTH, WIDTH)),
            vm((LENGTH, WIDTH)), vm((LENGTH, WIDTH)), vm((WIDTH, WIDTH)),
            vm((LENGTH, 3 * WIDTH)), vm((LENGTH, WIDTH), F32), vm((HEADS, LENGTH), F32),
            vm(tables.shape[1:], tables.dtype), vm((PAD, 2 * WIDTH)), vm((HEADS, LENGTH), F32),
            vm((PAD, 2 * WIDTH), F32), DMA((80,)),
        ],
        "middle", 2 * LENGTH * WIDTH * 36 * WIDTH, 80 << 20,
    )


def feed_back_kernel(
    sec, g, slope, middle, mixed, attended, totals, table, other, weight, pack, pack2, wo, wo2,
    we, we2, wr, wr2,
    grad_middle, grad_out, centres, payload,
    g_v, s_v, mid_v, q_v, at_v, to_v, tp_v, t_v, p_v, wo_v, we_v, wr_v, go_v, c_v, gt_v, gt0_v,
    pw_v, pay_v, sems,
):
    own = sec[0] == 0
    sem = Sems(sems)
    gs = rows_in(g, g_v, sem, 2, start=False)
    wrs = picked((wr, wr2), wr_v, sem, own, 0, 8)
    wes = picked((we, we2), we_v, sem, own, 1, 8)
    begin(gs[:1])
    parts = []
    for c in range(8):
        cols = tile(c, 512)
        parts.append([wrs[c], Copy(slope.at[:, cols], s_v.at[:, cols], sem()), wes[c]])
    begin(parts[0])
    wait(gs[:1])
    for c in range(1, 8):
        begin(parts[c])
    before = [
        gs[1].start(),
        picked((pack, pack2), p_v, sem, own)[0].start(),
        Copy(middle, mid_v, sem()).start(),
        picked((wo, wo2), wo_v, sem, own)[0].start(),
    ]
    later = [
        Copy(mixed.at[:, :WIDTH], q_v, sem()).start(),
        Copy(attended, at_v, sem()).start(),
        Copy(totals, to_v, sem()).start(),
        Copy(table.at[0], tp_v, sem()).start(),
        Copy(other, gt_v, sem()).start(),
        Copy(weight, pw_v, sem()).start(),
    ]
    groups = {}
    for c, size in ((0, 1), (1, 2), (3, 2), (5, 3)):
        groups[c] = [copy for part in parts[c : c + size] for copy in part]
    feed_back_phase(g_v, s_v, we_v, wr_v, wo_v, p_v, mid_v, go_v, groups, before)
    outs = [Copy(mid_v, grad_middle, sem()).start(), Copy(go_v, grad_out, sem()).start()]
    wait(later)
    join_table(tp_v, t_v)
    prefix_back(q_v, go_v, at_v, to_v, c_v, t_v, gt0_v)
    outs.append(Copy(c_v, centres, sem()).start())
    pack_payload((gt0_v, gt_v), pw_v, pay_v)
    outs.append(Copy(pay_v, payload, sem()).start())
    wait(outs)


def feed_back(sec, g, slope, middle, mixed, attended, totals, table, other, weight, packs, wo, we, wr):
    size = weight.shape[1]
    if weight.shape[2] == 128:
        payload = ((weight.shape[0], 2 * PAD + PAD * size // 128, 128), BF)
    else:
        payload = ((3 * PAD, 2 * WIDTH), F32)
    return call(
        feed_back_kernel,
        (
            sec, g, slope, middle, mixed, attended, totals, table, other, weight, *packs, *wo,
            *we, *wr,
        ),
        [SMEM] + [ANY] * 17,
        [((LENGTH, WIDTH), F32), ((LENGTH, WIDTH), BF), ((HEADS, LENGTH), F32), payload],
        [
            vm((LENGTH, WIDTH)), vm((LENGTH, FF)), vm((LENGTH, WIDTH), F32), vm((LENGTH, WIDTH)),
            vm((LENGTH, WIDTH)), vm((HEADS, LENGTH), F32), vm(table.shape[1:], table.dtype),
            vm((PAD, 2 * WIDTH)), vm((16, 1024), F32),
            vm((WIDTH, WIDTH)), vm((WIDTH, FF)), vm((FF, WIDTH)),
            vm((LENGTH, WIDTH)), vm((HEADS, LENGTH), F32), vm((PAD, 2 * WIDTH), F32),
            vm((PAD, 2 * WIDTH), F32), vm(weight.shape), vm(*payload), DMA((48,)),
        ],
        "feed_back", 2 * LENGTH * WIDTH * 9 * WIDTH, 40 << 20,
    )


def last_kernel(
    sec, lens, mixed, grad_out, totals, centres, table, x, grad_middle, grad1, keep, other,
    pack, pack2, w, w2,
    layer_out, input_grad, send,
    m_v, go_v, to_v, c_v, tp_v, t_v, gm_v, k_v, v_v, b_v, x_v, mid_v, p_v, w_v, o_v, sems,
):
    own = sec[0] == 0
    sem = Sems(sems)
    pairs = ((table.at[0], tp_v), (totals, to_v), (centres, c_v))
    copies = [Copy(a, b, sem()).start() for a, b in pairs]
    blocks = LENGTH // QB
    queries = rows_of(mixed, m_v, sem, blocks)
    outs_in = rows_of(grad_out, go_v, sem, blocks)
    for block in range(blocks):
        queries(block).start()
        outs_in(block).start()
    later = picked((pack, pack2), p_v, sem, own) + picked((w, w2), w_v, sem, own)
    later += [Copy(x.at[sec[0]], x_v, sem()), Copy(grad_middle, mid_v, sem())]
    ins = [
        Copy(keep, b_v.at[0], sem()), Copy(other, b_v.at[1], sem()), Copy(grad1, b_v.at[2], sem())
    ]
    outs = [
        Copy(b_v.at[0], layer_out.at[sec[0]], sem()),
        Copy(b_v.at[1], layer_out.at[1 - sec[0]], sem()),
    ]
    grad1_sem, base = sem(), sem.used
    grad1_outs = [
        pltpu.make_async_copy(b_v.at[2], target, grad1_sem) for target in (send, input_grad.at[1])
    ]
    wait(copies)
    join_table(tp_v, t_v)

    def arrive(block):
        queries(block).wait()
        outs_in(block).wait()

        @pl.when(block == 1)
        def _():
            begin(later)

        @pl.when(block == 3)
        def _():
            begin(ins)

        @pl.when(block == 5)
        def _():
            wait(ins)
            begin(outs)
            pl.when(own)(grad1_outs[0].start)
            pl.when(jnp.logical_not(own))(grad1_outs[1].start)

    attend_back(m_v, go_v, to_v, c_v, t_v, lens, sec[0], gm_v, (k_v, v_v), arrive)
    wait(later)

    def grad0(r):
        rows = tile(r, 256)
        return [
            pltpu.make_async_copy(o_v.at[rows], target.at[rows], sems.at[base + r])
            for target in (input_grad.at[0], send)
        ]

    def done(r):
        pl.when(own)(grad0(r)[0].start)
        pl.when(jnp.logical_not(own))(grad0(r)[1].start)

    mix_back_phase(gm_v, w_v, x_v, mid_v, p_v, o_v, lambda r: None, done)
    wait(outs)
    grad1_outs[0].wait()
    for r in range(4):
        grad0(r)[0].wait()


def last_part(sec, lens, mixed, grad_out, totals, centres, table, x, grad_middle, outs, packs, wm):
    return call(
        last_kernel,
        (sec, lens, mixed, grad_out, totals, centres, table, x, grad_middle, *outs, *packs, *wm),
        [SMEM, SMEM] + [ANY] * 14,
        [((2, LENGTH, WIDTH), BF), ((2, LENGTH, WIDTH), BF), ((LENGTH, WIDTH), BF)],
        [
            vm((LENGTH, 3 * WIDTH)), vm((LENGTH, WIDTH)), vm((HEADS, LENGTH), F32),
            vm((HEADS, LENGTH), F32), vm(table.shape[1:], table.dtype), vm((PAD, 2 * WIDTH)),
            vm((LENGTH, 3 * WIDTH)), vm((LENGTH, WIDTH), F32), vm((LENGTH, WIDTH), F32),
            vm((3, LENGTH, WIDTH)), vm((LENGTH, WIDTH)), vm((LENGTH, WIDTH), F32),
            vm((16, 1024), F32), vm((WIDTH, 3 * WIDTH)), vm((LENGTH, WIDTH)), DMA((48,)),
        ],
        "last", 2 * LENGTH * WIDTH * 13 * WIDTH, 50 << 20,
    )


def place_kernel(sec, other, grads, out, b_v, sems):
    parts = rows_in(other, b_v, Sems(sems.at[pl.ds(0, 4)]), start=False)
    target = out.at[1 - sec[0]]
    outs = rows_in(b_v, target, Sems(sems.at[pl.ds(4, 4)]), start=False)
    begin(parts)
    for r in range(4):
        parts[r].wait()
        outs[r].start()
    wait(outs)


def place(sec, other, grads):
    return pl.pallas_call(
        place_kernel,
        in_specs=[SMEM, ANY, ANY],
        out_specs=ANY,
        out_shape=jax.ShapeDtypeStruct(grads.shape, grads.dtype),
        scratch_shapes=[vm((LENGTH, WIDTH)), DMA((8,))],
        input_output_aliases={2: 0},
        compiler_params=pltpu.CompilerParams(vmem_limit_bytes=62 << 20),
        cost_estimate=pl.CostEstimate(flops=0, bytes_accessed=4 << 20, transcendentals=0),
        name="place",
    )(sec, other, grads)


def prefix_kernel(parts, activity, embed, hidden, ge, gw, gb, gpw, gpb):
    total = parts[0].astype(F32)
    for index in range(1, parts.shape[0]):
        total = total + parts[index].astype(F32)
    act = activity[...]
    share = [total[(2 + k) * PAD : (3 + k) * PAD] for k in range(act.shape[1] // 128)]
    pre = jnp.concatenate(share, 1) * (1.0 - act * act)
    pre = jnp.where(lax.broadcasted_iota(jnp.int32, pre.shape, 0) < PRE, pre, 0.0)
    high, low = split(pre)
    gb[...] = jnp.sum(pre, axis=0, keepdims=True)
    gw[...] = dot_tn(embed[...], high) + dot_tn(embed[...], low)
    ge[...] = dot_nt(high, hidden[...]) + dot_nt(low, hidden[...])
    mine = total[:PAD] + total[PAD : 2 * PAD]
    mine = jnp.where(lax.broadcasted_iota(jnp.int32, mine.shape, 0) < PRE, mine, 0.0)
    high, low = split(mine)
    rounded = act.astype(BF)
    size = gpw.shape[1]
    gpw[...] = (dot_tn(rounded, high) + dot_tn(rounded, low))[:, :size]
    gpb[...] = jnp.sum(mine, axis=0, keepdims=True)[:, :size]


def prefix_grads(parts, activity, embed, hidden, share):
    size = activity.shape[1]
    return call(
        prefix_kernel,
        (parts, activity, embed, hidden),
        [VMEM] * 4,
        [
            ((PAD, WIDTH), F32), ((WIDTH, size), F32), ((1, size), F32), ((size, share), F32),
            ((1, share), F32),
        ],
        [],
        "prefix_grads", 1 << 30, 10 << 20,
        out_specs=[VMEM] * 5,
    )


def per_device(
    inputs, cotangent, doc_lengths, attend_gain, attend_bias, mixing_weight, mixing_bias,
    output_weight, output_bias, feed_gain, feed_bias, expand_weight, expand_bias, reduce_weight,
    reduce_bias, prefix_embed, hidden_weight, hidden_bias, prefix_weight, prefix_bias,
):
    section = lax.axis_index("section")
    sec = section.astype(jnp.int32).reshape(1)
    everyone = ("section", "dp")
    places = lax.axis_size("dp")
    swap = lambda value: lax.ppermute(value, "section", [(0, 1), (1, 0)])
    x = inputs.reshape(2, LENGTH, WIDTH)
    cot = cotangent.reshape(2, LENGTH, WIDTH)
    lens = doc_lengths.reshape(2, DOCS)
    share = prefix_weight.shape[2]

    wm, wo, we, wr = mixing_weight[0], output_weight[0], expand_weight[0], reduce_weight[0]
    wm2, wo2 = swap(wm), swap(wo)
    vectors = (
        attend_gain, attend_bias, mixing_bias, output_bias, feed_gain, feed_bias, expand_bias,
        reduce_bias,
    )
    pack, activity, embed, part = call(
        prologue_kernel,
        (prefix_embed, hidden_weight, hidden_bias, prefix_weight[0], prefix_bias, *vectors),
        [VMEM] * 13,
        [
            ((16, 1024), F32), ((PAD, hidden_weight.shape[1]), F32), ((PAD, WIDTH), BF),
            ((2 * places, PAD, share), BF),
        ],
        [vm((PAD, WIDTH), F32)],
        "prologue", 1 << 24, 2 << 20,
        out_specs=[VMEM] * 4,
    )
    pack2 = swap(pack)

    tables = lax.all_to_all(part, everyone, 0, 0)
    tables = tables.reshape(2, places, PAD, share)
    if share % 128:
        tables = tables.transpose(0, 2, 1, 3).reshape(2, 1, PAD, 2 * WIDTH)
    full = lax.all_gather(prefix_weight[0], everyone, axis=0)
    if share != 128:
        full = full.reshape(2, places, -1, share).transpose(0, 2, 1, 3)
        full = full.reshape(2, -1, 2 * WIDTH)
    wm2, wo2, pack2, tables = lax.optimization_barrier((wm2, wo2, pack2, tables))
    packs = (pack, pack2)
    we_in, wr_in, wm2 = lax.optimization_barrier((we, wr, wm2))
    we2, wr2 = swap(we_in), swap(wr_in)
    wms, wos, wes, wrs = (wm, wm2), (wo, wo2), (we, we2), (wr, wr2)

    mixed, attended, totals = mix_attend(sec, lens, x, tables, packs, wms)
    keep, send, grad1, middle, slope, table_grad1 = middle_part(
        sec, lens, x, attended, tables, cot, packs, wms, wos, wes, wrs
    )
    other = swap(send)
    grad_middle, grad_out, centres, payload = feed_back(
        sec, grad1, slope, middle, mixed, attended, totals, tables, table_grad1, full, packs,
        wos, wes, wrs,
    )

    if share != 128:
        table_grads = jnp.stack(split(payload[: 2 * PAD].reshape(2, PAD, places, share)), 0)
        table_grads = table_grads.transpose(1, 3, 0, 2, 4).reshape(2 * places, 2 * PAD, share)
        table_grads = jnp.pad(table_grads, ((0, 0), (0, 0), (0, 128 - share)))
        units = payload[2 * PAD :, : activity.shape[1]].reshape(PAD, -1, 128).transpose(1, 0, 2)
        units = jnp.broadcast_to(units.astype(BF).reshape(1, -1, 128), (2 * places, units.size // 128, 128))
        payload = jnp.concatenate([table_grads, units], 1)
    parts = lax.all_to_all(payload, everyone, 0, 0)
    layer_out, grads, send = last_part(
        sec, lens, mixed, grad_out, totals, centres, tables, x, grad_middle,
        (grad1, keep, other), packs, wms,
    )
    parts, send, grads = lax.optimization_barrier((parts, send, grads))
    other = swap(send)
    ge, gw, gb, gpw, gpb = prefix_grads(parts, activity, embed, hidden_weight, share)
    input_grad = place(sec, other, grads)
    shape = (1, 2, 1, LENGTH, WIDTH)
    return (
        layer_out.reshape(shape), input_grad.reshape(shape), ge[:PRE], gw, gb[0], gpw[None], gpb
    )


def solution(mesh):
    in_specs = (
        P(None, "dp", None, None),
        P(None, "dp", None, None),
        P(None, "dp", None),
        P("section", None),
        P("section", None),
        P("section", None, None),
        P("section", None),
        P("section", None, None),
        P("section", None),
        P("section", None),
        P("section", None),
        P("section", None, None),
        P("section", None),
        P("section", None, None),
        P("section", None),
        P(),
        P(),
        P(),
        P("section", None, "dp"),
        P("section", "dp"),
    )
    out_specs = (
        P("section", None, "dp", None, None),
        P("section", None, "dp", None, None),
        P(),
        P(),
        P(),
        P("section", None, "dp"),
        P("section", "dp"),
    )
    return jax.shard_map(
        per_device, mesh=mesh, in_specs=in_specs, out_specs=out_specs, check_vma=False
    )
```
